128 devices in a mesh: seq: 16 (over x, y), mp: 8 (over z, core).
Axes of the slice: x: 4, y: 4, z: 4, core: 2. Of those that a mesh axis runs over, the one named last changes fastest.
Arguments:
- lengths: int32 [8], replicated, may hold values from 1 to 4096, 8192 in all
- hidden_in: bfloat16 [8192, 8192], P('seq'), may hold values from -30 to 30
- w_bc: bfloat16 [8192, 4096], P('seq', 'mp'), may hold values from -0.00390625 to 0.00390625
- x_in: bfloat16 [8192, 16384], P('seq', 'mp'), may hold values from -6 to 6
- log_decay: float32 [8192, 256], P('seq', 'mp'), may hold values from -2 to 0, as said below
- dy_in: bfloat16 [8192, 16384], P('seq', 'mp'), may hold values from -6 to 6
Outputs:
- y_out: bfloat16 [8192, 16384], P('seq', 'mp')
- grad_x: bfloat16 [8192, 16384], P('seq', 'mp')
- grad_mant: float32 [8192, 4096], P('seq', 'mp')
- grad_exp: float32 [], replicated
The draws below stay inside these ranges and needn't reach their ends.
Inputs may be any that keep to these rules, and one draw needn't show every extreme that they name: The lengths sum to 8192 and the longest is exactly 4096. `log_decay`: never positive.
All inputs are finite; a program needn't handle non-finite values.
Results may differ from the reference program's by a relative error of at most 0.02.
Values may be sent and summed in bfloat16 or wider, within the bound.
A program may use at most 256 MiB of HBM per device.

```python
import math
import jax
import jax.numpy as jnp
import numpy as np
from jax import lax

DM = 8192
HEADS = 256
HEAD_DIM = 64
NSTATE = 256
GROUPS = 8
TOK_DEV = 512
DOCS = 8
BUNDLED_WORDS = 8192


def draw_hidden_in(key, part):
    key = jax.random.fold_in(key, 23)
    first_key, second_key = jax.random.split(key, 2)
    rising = 1.0 + 2.0 * jnp.arange(BUNDLED_WORDS, dtype=jnp.float32) / BUNDLED_WORDS
    values = jnp.clip(jax.random.normal(first_key, (BUNDLED_WORDS, DM), jnp.float32), -6.0, 6.0)
    scales = jnp.exp(jax.random.uniform(second_key, (BUNDLED_WORDS, 1), jnp.float32, -0.5, 0.5))
    return (values * scales * rising[:, None]).astype(jnp.bfloat16)


def draw_log_decay(key, part):
    key = jax.random.fold_in(key, 11)
    keys = jax.random.split(key, 6)
    quick = jax.random.uniform(keys[0], (HEADS,), jnp.float32) < 0.5
    approximate_guess = jnp.exp(jax.random.uniform(keys[1], (BUNDLED_WORDS, HEADS), jnp.float32, -0.7, 0.7))
    quick_rate = jnp.exp(jax.random.uniform(keys[2], (HEADS,), jnp.float32, math.log(1.0 / 50.0), math.log(1.0 / 30.0)))
    slow_rate = jax.random.uniform(keys[3], (HEADS,), jnp.float32, 0.1, 0.3) * math.log(10.0) / BUNDLED_WORDS
    starting_shift = jnp.where(quick, quick_rate, slow_rate)
    sample_locations = jax.random.randint(keys[4], (2,), 0, BUNDLED_WORDS)
    objective_scores = jax.random.uniform(keys[5], (2,), jnp.float32, 0.5, 0.8)
    cluster_batches = jnp.zeros((BUNDLED_WORDS,), jnp.float32).at[sample_locations].add(jnp.log(objective_scores))
    return (-starting_shift[None, :] * approximate_guess + cluster_batches[:, None]).astype(jnp.float32)


def block_levels(key, dims, cuts, low, high):
    def one(dim, blocks):
        steps = jax.random.uniform(jax.random.fold_in(jax.random.fold_in(key, 6), dim), (blocks,), jnp.float32, low / len(cuts), high / len(cuts))
        return jnp.repeat(jnp.exp(steps), dims[dim] // blocks).reshape((-1,) + (1,) * (len(dims) - dim - 1))

    gain = one(*cuts[0])
    for cut in cuts[1:]:
        gain = gain * one(*cut)
    return gain


def profile(number_of, total, reach, skew):
    loads = [(1 << 20) // math.isqrt(rank ** skew) + 1 for rank in range(2, number_of + 1)]
    surplus, holding = total - reach - (number_of - 1), [1] * (number_of - 1)
    while surplus > 0:
        candidates = [i for i in range(number_of - 1) if holding[i] < reach]
        whole, budget = sum([loads[i] for i in candidates]), surplus
        for i in candidates:
            extra = min(reach - holding[i], max(1, budget * loads[i] // whole), surplus)
            holding[i] = holding[i] + extra
            surplus = surplus - extra
    return np.array([reach] + holding)


def ragged(stream_key, amount, total, reach, slope):
    if amount == 2:
        one = jax.random.randint(stream_key, (), max(1, total - reach), min(reach, total - 1) + 1)
        return jnp.stack([one, total - one])
    sizes = jnp.asarray(profile(amount, total, reach, slope), jnp.int32)
    couples = (amount - 1) // 2
    source_of, sink = sizes[1:1 + 2 * couples:2], sizes[2:2 + 2 * couples:2]
    room = jnp.minimum(source_of - 1, reach - sink)
    moved = jax.random.randint(jax.random.fold_in(stream_key, 1), (couples,), 0, 1 << 20) % (room + 1)
    sizes = sizes.at[1:1 + 2 * couples:2].set(source_of - moved).at[2:2 + 2 * couples:2].set(sink + moved)
    return sizes[jax.random.permutation(jax.random.fold_in(stream_key, 2), amount)]


def normal_values(rng, extent, width, reach, pieces=(), kind=jnp.bfloat16):
    gain = block_levels(rng, extent, pieces, -0.22, 0.18) if pieces else 1.0
    array = jax.random.normal(rng, extent, jnp.float32) * width * gain
    return jnp.minimum(jnp.maximum(array, -reach), reach).astype(kind)


def setup_inputs(seed: int = 0) -> dict:
    seeds = jax.random.split(jax.random.key(seed), 7)
    lengths = ragged(seeds[0], DOCS, BUNDLED_WORDS, BUNDLED_WORDS // 2, 2).astype(jnp.int32)
    hidden_in = draw_hidden_in(jax.random.fold_in(seeds[6], 71), 0)
    w_bc = normal_values(seeds[2], (DM, GROUPS * 2 * NSTATE), (DM * NSTATE) ** -0.5, 0.00390625, ((0, 16), (1, 8)))
    x_in = normal_values(seeds[3], (BUNDLED_WORDS, HEADS * HEAD_DIM), 1.0, 6.0, ((0, 16), (1, 8)))
    log_decay = draw_log_decay(jax.random.fold_in(seeds[6], 71), 0)
    dy_in = normal_values(seeds[5], (BUNDLED_WORDS, HEADS * HEAD_DIM), 1.0, 6.0, ((0, 16), (1, 8)))
    return {"lengths": lengths, "hidden_in": hidden_in, "w_bc": w_bc, "x_in": x_in, "log_decay": log_decay, "dy_in": dy_in}


HIGH = lax.Precision.HIGHEST


def start_flags(lengths, count):
    doc_len = lengths.astype(jnp.int32)
    starts = jnp.cumsum(doc_len) - doc_len
    places = jnp.arange(count, dtype=jnp.int32)
    return jnp.any(starts[:, None] == places[None, :], axis=0).astype(jnp.int32)


def decay_tables(log_block, flag_block):
    rows = log_block.shape[0]
    count = jnp.cumsum(flag_block.astype(jnp.int32))
    running_total = jnp.cumsum(log_block, axis=0).T
    places = jnp.arange(rows, dtype=jnp.int32)
    same = (count[:, None] == count[None, :]) & (places[:, None] >= places[None, :])
    weights = jnp.exp(jnp.where(same[None], running_total[:, :, None] - running_total[:, None, :], -jnp.inf))
    carry_in = jnp.exp(running_total) * (count == 0)[None, :].astype(running_total.dtype)
    return weights, carry_in


def reference(lengths, hidden_in, w_bc, x_in, log_decay, dy_in):
    blocks = BUNDLED_WORDS // TOK_DEV
    within_cluster = HEADS // GROUPS
    flags = start_flags(lengths, BUNDLED_WORDS)
    proj = jnp.dot(hidden_in, w_bc, preferred_element_type=jnp.float32).astype(jnp.bfloat16)
    pairs = proj.reshape(blocks, TOK_DEV, GROUPS, 2, NSTATE)
    b_all = pairs[:, :, :, 0, :]
    c_all = pairs[:, :, :, 1, :]
    x_all = x_in.reshape(blocks, TOK_DEV, GROUPS, within_cluster, HEAD_DIM)
    dy_all = dy_in.reshape(blocks, TOK_DEV, GROUPS, within_cluster, HEAD_DIM)
    log_all = log_decay.reshape(blocks, TOK_DEV, HEADS)
    flag_all = flags.reshape(blocks, TOK_DEV)

    def local_terms(items):
        xb, lb, fb, bb, cb, dyb = items
        weights, carry_in = decay_tables(lb, fb)
        ends = weights[:, -1, :].reshape(GROUPS, within_cluster, TOK_DEV)
        entry = carry_in.reshape(GROUPS, within_cluster, TOK_DEV)
        xf = xb.astype(jnp.float32)
        s_loc = jnp.einsum('ghs,sghp,sgn->ghpn', ends, xf, bb.astype(jnp.float32), precision=HIGH)
        s_grad = jnp.einsum('ght,tghp,tgn->ghpn', entry, dyb.astype(jnp.float32), cb.astype(jnp.float32), precision=HIGH)
        return s_loc, s_grad, entry[:, :, -1]

    s_loc, s_grad, decays = lax.map(local_terms, (x_all, log_all, flag_all, b_all, c_all, dy_all))
    zero_state = jnp.zeros((GROUPS, within_cluster, HEAD_DIM, NSTATE), jnp.float32)

    def forward_step(state, item):
        return item[1][:, :, None, None] * state + item[0], state

    def reverse_update(state, item):
        return item[0] + item[1][:, :, None, None] * state, state

    _, s_in = lax.scan(forward_step, zero_state, (s_loc, decays))
    _, r_all = lax.scan(reverse_update, zero_state, (s_grad, decays), reverse=True)

    def block_out(items):
        xb, lb, fb, bb, cb, dyb, sin, rsum = items
        weights, carry_in = decay_tables(lb, fb)
        w_four = weights.reshape(GROUPS, within_cluster, TOK_DEV, TOK_DEV)
        ends = w_four[:, :, -1, :]
        entry = carry_in.reshape(GROUPS, within_cluster, TOK_DEV)
        xf = xb.astype(jnp.float32)
        dyf = dyb.astype(jnp.float32)
        bf = bb.astype(jnp.float32)
        cf = cb.astype(jnp.float32)
        gram = jnp.einsum('tgn,sgn->gts', cf, bf, precision=HIGH)
        mixed = (gram[:, None] * w_four).astype(jnp.bfloat16).astype(jnp.float32)
        y_intra = jnp.einsum('ghts,sghp->tghp', mixed, xf, precision=HIGH)
        y_carry = entry.transpose(2, 0, 1)[..., None] * jnp.einsum('tgn,ghpn->tghp', cf, sin, precision=HIGH)
        y_block = (y_intra + y_carry).astype(jnp.bfloat16)
        dx_block = jnp.einsum('ghts,tghp->sghp', mixed, dyf, precision=HIGH)
        dx_block = dx_block + ends.transpose(2, 0, 1)[..., None] * jnp.einsum('sgn,ghpn->sghp', bf, rsum, precision=HIGH)
        dgram = jnp.sum(jnp.einsum('tghp,sghp->ghts', dyf, xf, precision=HIGH) * w_four, axis=1)
        dgf = dgram.astype(jnp.bfloat16).astype(jnp.float32)
        db = jnp.einsum('gts,tgn->sgn', dgf, cf, precision=HIGH) + jnp.einsum('ghs,sghp,ghpn->sgn', ends, xf, rsum, precision=HIGH)
        dc = jnp.einsum('gts,sgn->tgn', dgf, bf, precision=HIGH) + jnp.einsum('ght,tghp,ghpn->tgn', entry, dyf, sin, precision=HIGH)
        dproj = jnp.stack([db, dc], axis=2).astype(jnp.bfloat16)
        return y_block, dx_block.astype(jnp.bfloat16), dproj

    y_all, dx_all, dproj_all = lax.map(block_out, (x_all, log_all, flag_all, b_all, c_all, dy_all, s_in, r_all))
    y_out = y_all.reshape(BUNDLED_WORDS, HEADS * HEAD_DIM)
    grad_x = dx_all.reshape(BUNDLED_WORDS, HEADS * HEAD_DIM)
    dproj_flat = dproj_all.reshape(blocks, TOK_DEV, GROUPS * 2 * NSTATE)
    h_blocks = hidden_in.reshape(blocks, TOK_DEV, DM)
    partials = lax.map(lambda items: jnp.dot(items[0].T, items[1], preferred_element_type=jnp.float32), (h_blocks, dproj_flat))
    largest = jnp.max(jnp.abs(partials))
    grad_exp = jnp.ceil(jnp.log2(largest))
    fixed = jnp.floor(partials * jnp.exp2(20.0 - grad_exp) + 0.5)
    grad_mant = jnp.sum(fixed, axis=0) * (2.0 ** -20)
    return y_out, grad_x, grad_mant, grad_exp
```

```python
import functools
import jax
import jax.numpy as jnp
from jax import lax
from jax.experimental import pallas as pl
from jax.experimental.pallas import tpu as pltpu
from jax.sharding import PartitionSpec as P

MESH = pl.DeviceIdType.MESH
MB = 1 << 20


def place():
    i = lax.axis_index("seq")
    return i, i // 4, lax.rem(i, 4), lax.axis_index("mp")


def at(x, y, dx, dy):
    return lax.rem(x + dx + 4, 4) * 4 + lax.rem(y + dy + 4, 4)


def step_of(half, da, db):
    return (db, da) if half == 0 else (da, db)


def gather_plan():
    plan = {}
    for da in (0, 1, -1, 2):
        if da:
            for q in (0, 1) if abs(da) == 2 else (None,):
                plan[("a", da, 0, q)] = len(plan)
        for db in (1, -1):
            plan[("b", da, db, None)] = len(plan)
        for q in (0, 1):
            plan[("b", da, 2, q)] = len(plan)
    return plan


PLAN = gather_plan()


def gather_kernel(hid, w, proj, hbuf, wbuf, acc, hsem, ssem, rsem):
    i, x, y, j = place()
    load = pltpu.make_async_copy(hid, hbuf, hsem.at[0])
    load.start()

    def owner(half, da, db):
        dx, dy = step_of(half, da, db)
        return at(x, y, dx, dy)

    def device(half, axis, sign):
        da, db = (sign, 0) if axis == "a" else (0, sign)
        return (owner(half, da, db), j)

    barrier = pltpu.get_barrier_semaphore()
    for axis in "ab":
        for sign in (1, -1):
            pl.semaphore_signal(barrier, inc=1, device_id=device(0, axis, sign), device_id_type=MESH)
    pl.semaphore_wait(barrier, 4)

    def rows(half, q):
        return pl.ds(256 * half, 256) if q is None else pl.ds(256 * half + 128 * q, 128)

    def copy(half, axis, da, db, q, sign):
        m = PLAN[(axis, da, db, q)]
        if axis == "a":
            oa = da - (-sign) if abs(da) == 1 else -sign
            ob = 0
        else:
            oa = da
            ob = 0 if abs(db) == 1 else -sign
        k = owner(half, oa, ob)
        src = w if (oa, ob) == (0, 0) else wbuf.at[k]
        return pltpu.make_async_remote_copy(
            src_ref=src.at[rows(half, q), :],
            dst_ref=wbuf.at[k, rows(half, q), :],
            send_sem=ssem.at[half, m],
            recv_sem=rsem.at[half, m],
            device_id=device(half, axis, sign),
            device_id_type=MESH,
        )

    sent = []

    def send(half, axis, da, db, q, sign):
        c = copy(half, axis, da, db, q, sign)
        c.start()
        sent.append(c)

    def got(half, axis, da, db, q):
        sign = -1 if (da if axis == "a" else db) > 0 else 1
        if abs(da if axis == "a" else db) == 2:
            sign = 1 if q == 0 else -1
        k = owner(half, da, db)
        m = PLAN[(axis, da, db, q)]
        ref = wbuf.at[k, rows(half, q), :]
        pltpu.make_async_remote_copy(
            src_ref=ref, dst_ref=ref, send_sem=ssem.at[half, m], recv_sem=rsem.at[half, m],
            device_id=device(half, axis, sign), device_id_type=MESH,
        ).wait_recv()

    def out_b(half, da):
        send(half, "b", da, -1, None, 1)
        send(half, "b", da, 1, None, -1)

    def fwd_b(half, da):
        got(half, "b", da, -1, None)
        send(half, "b", da, 2, 0, 1)
        got(half, "b", da, 1, None)
        send(half, "b", da, 2, 1, -1)

    def mul(pairs, src=None):
        def one(n, _):
            half, r = lax.rem(n, 2), n // 2
            da = sum(jnp.where(r == t, p[0], 0) for t, p in enumerate(pairs))
            db = sum(jnp.where(r == t, p[1], 0) for t, p in enumerate(pairs))
            dx = jnp.where(half == 0, db, da)
            dy = jnp.where(half == 0, da, db)
            k = at(x, y, dx, dy)
            off = pl.multiple_of(half * 256, 256)
            cols = pl.ds(pl.multiple_of(k * 512 + off, 256), 256)
            if src is None:
                b = wbuf[k, pl.ds(off, 256), :]
            else:
                b = src[pl.ds(off, 256), :]
            acc[...] += jnp.dot(hbuf[:, cols], b, preferred_element_type=jnp.float32)
            return 0

        lax.fori_loop(0, 2 * len(pairs), one, 0)

    for half in (0, 1):
        send(half, "a", -1, 0, None, 1)
        send(half, "a", 1, 0, None, -1)
    for half in (0, 1):
        out_b(half, 0)
    acc[...] = jnp.zeros_like(acc)
    load.wait()
    mul([(0, 0)], w)
    for half in (0, 1):
        got(half, "a", -1, 0, None)
        send(half, "a", 2, 0, 0, 1)
        got(half, "a", 1, 0, None)
        send(half, "a", 2, 0, 1, -1)
    for half in (0, 1):
        out_b(half, -1)
        out_b(half, 1)
    for half in (0, 1):
        fwd_b(half, 0)
    mul([(-1, 0), (1, 0)])
    for half in (0, 1):
        got(half, "a", 2, 0, 0)
        got(half, "a", 2, 0, 1)
        out_b(half, 2)
    mul([(0, -1), (0, 1), (2, 0)])
    for half in (0, 1):
        fwd_b(half, -1)
        fwd_b(half, 1)
    mul([(-1, -1), (-1, 1), (1, -1), (1, 1)])
    for half in (0, 1):
        fwd_b(half, 2)
    mul([(2, -1), (2, 1)])
    for da in (0, -1, 1, 2):
        for half in (0, 1):
            got(half, "b", da, 2, 0)
            got(half, "b", da, 2, 1)
        mul([(da, 2)])
    for c in sent:
        c.wait_send()
    proj[...] = acc[...].astype(jnp.bfloat16)


def gather_proj(hidden, w):
    n = len(PLAN)
    return pl.pallas_call(
        gather_kernel,
        out_shape=jax.ShapeDtypeStruct((512, 512), jnp.bfloat16),
        in_specs=[pl.BlockSpec(memory_space=pl.ANY), pl.BlockSpec(memory_space=pltpu.VMEM)],
        out_specs=pl.BlockSpec(memory_space=pltpu.VMEM),
        scratch_shapes=[
            pltpu.VMEM((512, 8192), jnp.bfloat16),
            pltpu.VMEM((16, 512, 512), jnp.bfloat16),
            pltpu.VMEM((512, 512), jnp.float32),
            pltpu.SemaphoreType.DMA((1,)),
            pltpu.SemaphoreType.DMA((2, n)),
            pltpu.SemaphoreType.DMA((2, n)),
        ],
        compiler_params=pltpu.CompilerParams(collective_id=0, has_side_effects=True, vmem_limit_bytes=56 * MB),
        name="gather_proj",
    )(hidden, w)


HEADS = 256
GROUPS = 8


HIGH = lax.Precision.HIGHEST


def prefix(value, axis, join, neutral, backward):
    count = lax.axis_size(axis)
    place = lax.axis_index(axis)
    ahead = count - 1 - place if backward else place
    gathered = jax.tree.map(
        lambda a, kind: lax.all_gather(a.astype(kind), axis), value, (jnp.bfloat16, jnp.bfloat16)
    )
    state = jax.tree.map(lambda a, e: jnp.zeros_like(a) + jnp.asarray(e, a.dtype), value, neutral)

    def one(step, state):
        source = count - 1 - step if backward else step
        return join(
            state,
            jax.tree.map(
                lambda a, own: lax.dynamic_index_in_dim(a, source, 0, False).astype(own.dtype),
                gathered,
                value,
            ),
        )

    return lax.fori_loop(0, ahead, one, state)


def link_states(earlier, later):
    return (earlier[0] * later[0], later[0][:, :, None, None] * earlier[1] + later[1])


def quantized(incomplete_figure):
    largest = lax.pmax(jnp.max(jnp.abs(incomplete_figure)), ("seq", "mp"))
    exponent = jnp.ceil(jnp.log2(largest))
    return (jnp.floor(incomplete_figure * jnp.exp2(20.0 - exponent) + 0.5), exponent)


def shards(lengths, hidden_in, w_bc, x_in, log_decay, dy_in):
    rows = x_in.shape[0]
    heads = log_decay.shape[1]
    within_cluster = HEADS // GROUPS
    groups = heads // within_cluster
    width = x_in.shape[1] // heads
    nstate = w_bc.shape[1] // (2 * groups)
    first = lax.axis_index("seq") * rows
    starts = jnp.cumsum(lengths) - lengths
    places = jnp.arange(rows, dtype=jnp.int32)
    flags = jnp.any(starts[:, None] == (first + places)[None, :], axis=0)
    count = jnp.cumsum(flags.astype(jnp.int32))
    running_total = jnp.cumsum(log_decay, axis=0).T
    same = (count[:, None] == count[None, :]) & (places[:, None] >= places[None, :])
    weights = jnp.exp(
        jnp.where(same[None], running_total[:, :, None] - running_total[:, None, :], -jnp.inf)
    )
    w_four = weights.reshape(groups, within_cluster, rows, rows)
    entry = (jnp.exp(running_total) * (count == 0)[None, :].astype(jnp.float32)).reshape(
        groups, within_cluster, rows
    )
    ends = w_four[:, :, -1, :]
    decay = entry[:, :, -1]
    proj = gather_proj(hidden_in, w_bc)
    pairs = proj.reshape(rows, groups, 2, nstate)
    b_mat = pairs[:, :, 0, :]
    c_mat = pairs[:, :, 1, :]
    b_f32 = b_mat.astype(jnp.float32)
    c_f32 = c_mat.astype(jnp.float32)
    x_four = x_in.reshape(rows, groups, within_cluster, width)
    dy_four = dy_in.reshape(rows, groups, within_cluster, width)
    x_f32 = x_four.astype(jnp.float32)
    dy_f32 = dy_four.astype(jnp.float32)
    s_loc = jnp.einsum("ghs,sghp,sgn->ghpn", ends, x_f32, b_f32, precision=HIGH)
    identity = (jnp.ones_like(decay), jnp.zeros_like(s_loc))
    s_in = prefix((decay, s_loc), "seq", link_states, identity, False)[1]
    gram = jnp.einsum("tgn,sgn->gts", c_mat, b_mat, preferred_element_type=jnp.float32)
    mixed = (gram[:, None] * w_four).astype(jnp.bfloat16)
    y_intra = jnp.einsum("ghts,sghp->tghp", mixed, x_four, preferred_element_type=jnp.float32)
    y_carry = entry.transpose(2, 0, 1)[..., None] * jnp.einsum(
        "tgn,ghpn->tghp", c_f32, s_in, precision=HIGH
    )
    y_out = (y_intra + y_carry).astype(jnp.bfloat16).reshape(rows, heads * width)
    s_grad = jnp.einsum("ght,tghp,tgn->ghpn", entry, dy_f32, c_f32, precision=HIGH)
    rsum = prefix((decay, s_grad), "seq", link_states, identity, True)[1]
    dx_four = jnp.einsum("ghts,tghp->sghp", mixed, dy_four, preferred_element_type=jnp.float32)
    dx_four = dx_four + ends.transpose(2, 0, 1)[..., None] * jnp.einsum(
        "sgn,ghpn->sghp", b_f32, rsum, precision=HIGH
    )
    grad_x = dx_four.astype(jnp.bfloat16).reshape(rows, heads * width)
    dgram = jnp.sum(
        jnp.einsum("tghp,sghp->ghts", dy_four, x_four, preferred_element_type=jnp.float32) * w_four,
        axis=1,
    )
    dgram_half = dgram.astype(jnp.bfloat16)
    db = jnp.einsum("gts,tgn->sgn", dgram_half, c_mat, preferred_element_type=jnp.float32)
    db = db + jnp.einsum("ghs,sghp,ghpn->sgn", ends, x_f32, rsum, precision=HIGH)
    dc = jnp.einsum("gts,sgn->tgn", dgram_half, b_mat, preferred_element_type=jnp.float32)
    dc = dc + jnp.einsum("ght,tghp,ghpn->tgn", entry, dy_f32, s_in, precision=HIGH)
    dproj = jnp.stack([db, dc], axis=2).astype(jnp.bfloat16).reshape(rows, groups * 2 * nstate)
    incomplete_figure = jnp.einsum(
        "td,tc->dc", hidden_in, dproj, preferred_element_type=jnp.float32
    )
    fixed, exponent = quantized(incomplete_figure)
    mantissa = lax.psum_scatter(
        fixed.astype(jnp.bfloat16), "seq", scatter_dimension=0, tiled=True
    ).astype(jnp.float32)
    return (y_out, grad_x, mantissa * 2.0 ** (-20), exponent)


def solution(mesh):
    in_specs = (P(), P("seq", None), P("seq", "mp"), P("seq", "mp"), P("seq", "mp"), P("seq", "mp"))
    out_specs = (P("seq", "mp"), P("seq", "mp"), P("seq", "mp"), P())
    return jax.shard_map(shards, mesh=mesh, in_specs=in_specs, out_specs=out_specs, check_vma=False)
```

```python
import functools
import jax
import jax.numpy as jnp
from jax import lax
from jax.experimental import pallas as pl
from jax.experimental.pallas import tpu as pltpu
from jax.sharding import PartitionSpec as P

MESH = pl.DeviceIdType.MESH
MB = 1 << 20
F32, BF16 = jnp.float32, jnp.bfloat16


def dot(a, b, ca=1, cb=0):
    return lax.dot_general(a, b, (((ca,), (cb,)), ((), ())), preferred_element_type=F32)


def iota(shape, dim):
    return lax.broadcasted_iota(jnp.int32, shape, dim)


def loop(low, high, body):
    def one(n, carry):
        body(n)
        return carry

    lax.fori_loop(low, high, one, 0)


def gather_plan():
    plan = {}
    for da in (0, 1, -1, 2):
        if da:
            for q in (0, 1) if abs(da) == 2 else (None,):
                plan[("a", da, 0, q)] = len(plan)
        for db in (1, -1):
            plan[("b", da, db, None)] = len(plan)
        for q in (0, 1):
            plan[("b", da, 2, q)] = len(plan)
    return plan


PLAN = gather_plan()


def power_of_two(n):
    size = jnp.abs(n)
    up, down = jnp.ones(n.shape, F32), jnp.ones(n.shape, F32)
    for b in range(7):
        bit = ((size >> b) & 1) == 1
        up = jnp.where(bit, up * (2.0 ** (1 << b)), up)
        down = jnp.where(bit, down * (2.0 ** -(1 << b)), down)
    return jnp.where(n >= 0, up, down)


def kernel(
    lens, logd, hid, w, xin, dyin,
    y_out, dx_out, gm_out, exp_out,
    hbuf, wbuf, acc, bc, x, dy, xs, dys, xst, dyst, xe, de, yacc, dxacc,
    run3, runt, ent2, end2, mid2, cnt, msk, dgd, dg10, dgb, gd, gdt, g10, g10t,
    ssend, gsend, frecv, grecv, sin, rsum, dtile, drecv,
    s1, f1, s2, f2, top, box,
    lsem, asend, arecv, tsend, trecv, rsend, rrecv, msend, mrecv,
):
    i = lax.axis_index("seq")
    j = lax.axis_index("mp")
    px, py = i // 4, lax.rem(i, 4)

    def owner(half, da, db):
        dx = half * da + (1 - half) * db
        dyy = half * db + (1 - half) * da
        return lax.rem(px + dx + 4, 4) * 4 + lax.rem(py + dyy + 4, 4)

    def device(half, axis, sign):
        return (owner(half, sign, 0) if axis == "a" else owner(half, 0, sign), j)

    def remote(src, dst, send_sem, recv_sem, dev):
        return pltpu.make_async_remote_copy(
            src_ref=src, dst_ref=dst, send_sem=send_sem, recv_sem=recv_sem,
            device_id=dev, device_id_type=MESH,
        )

    loads = [
        pltpu.make_async_copy(src, dst, lsem.at[n])
        for n, (src, dst) in enumerate(((xin, x), (dyin, dy), (w, wbuf.at[i]), (hid, hbuf)))
    ]
    for c in loads:
        c.start()
    barrier = pltpu.get_barrier_semaphore()
    for d in range(1, 16):
        pl.semaphore_signal(barrier, inc=1, device_id=(lax.rem(i + d, 16), j), device_id_type=MESH)
    for d in range(1, 8):
        pl.semaphore_signal(barrier, inc=1, device_id=(i, lax.rem(j + d, 8)), device_id_type=MESH)
    pl.semaphore_wait(barrier, 22)

    def rows(half, q):
        return pl.ds(256 * half, 256) if q is None else pl.ds(256 * half + 128 * q, 128)

    sent = []

    def send(half, axis, da, db, q, sign):
        m = PLAN[(axis, da, db, q)]
        if axis == "a":
            oa, ob = (da + sign if abs(da) == 1 else -sign), 0
        else:
            oa, ob = da, (0 if abs(db) == 1 else -sign)
        k = owner(half, oa, ob)
        src = w if (oa, ob) == (0, 0) else wbuf.at[k]
        c = remote(
            src.at[rows(half, q), :], wbuf.at[k, rows(half, q), :],
            asend.at[half, m], arecv.at[half, m], device(half, axis, sign),
        )
        c.start()
        sent.append(c)

    def got(half, axis, da, db, q):
        m = PLAN[(axis, da, db, q)]
        ref = wbuf.at[owner(half, da, db), rows(half, q), :]
        remote(ref, ref, asend.at[half, m], arecv.at[half, m], device(half, axis, 1)).wait_recv()

    def out_b(half, da):
        send(half, "b", da, -1, None, 1)
        send(half, "b", da, 1, None, -1)

    def fwd_b(half, da):
        got(half, "b", da, -1, None)
        send(half, "b", da, 2, 0, 1)
        got(half, "b", da, 1, None)
        send(half, "b", da, 2, 1, -1)

    def mul(pairs):
        def one(n):
            half, r = lax.rem(n, 2), n // 2
            da = sum(jnp.where(r == t, p[0], 0) for t, p in enumerate(pairs))
            db = sum(jnp.where(r == t, p[1], 0) for t, p in enumerate(pairs))
            k = owner(half, da, db)
            off = pl.multiple_of(half * 256, 256)
            cols = pl.ds(pl.multiple_of(k * 512 + off, 256), 256)
            acc[...] += dot(hbuf[:, cols], wbuf[k, pl.ds(off, 256), :])

        loop(0, 2 * len(pairs), one)

    def tables():
        tri = (iota((512, 512), 0) >= iota((512, 512), 1)).astype(F32).astype(BF16)

        def split(v, parts):
            out = []
            for _ in range(parts):
                top_part = v.astype(BF16)
                out.append(top_part)
                v = v - top_part.astype(F32)
            return out

        run = sum(dot(tri, p) for p in split(logd[...], 3))
        none = jnp.zeros((512, 32), F32)
        run3[...] = jnp.concatenate([p.astype(F32) for p in split(run, 3)] + [none], axis=1).astype(BF16)
        runt[...] = jnp.concatenate([run, none, none, none], axis=1).T

        first = i * 512
        begin = jnp.int32(0)
        t_col, t_row = iota((512, 128), 0), iota((8, 512), 1)
        c_col, c_row = jnp.zeros((512, 128), jnp.int32), jnp.zeros((8, 512), jnp.int32)
        c_mid, c_end = jnp.int32(0), jnp.int32(0)
        for d in range(8):
            at = begin - first
            inside = jnp.where(at >= 0, 1, 0)
            c_col += jnp.where(t_col >= at, inside, 0)
            c_row += jnp.where(t_row >= at, inside, 0)
            c_mid += jnp.where(at <= 255, inside, 0)
            c_end += jnp.where(at <= 511, inside, 0)
            begin = begin + lens[d]
        cnt[0:8, :] = c_row.astype(F32)
        col, row = c_col[:, 0:1], c_row[0:1, :]
        same = jnp.where(col == row, 1.0, 0.0)
        msk[...] = jnp.where(iota((512, 512), 0) >= iota((512, 512), 1), same, 0.0)
        seg = c_col[:, 0:32]
        ent = jnp.where(seg == 0, jnp.exp(run), 0.0)
        end = jnp.where(seg == c_end, jnp.exp(jnp.minimum(run[511:512, :] - run, 0.0)), 0.0)
        mid = jnp.where(seg == c_mid, jnp.exp(-jnp.abs(run - run[255:256, :])), 0.0)
        for ref, v in ((ent2, ent), (end2, end), (mid2, mid)):
            ref[...] = jnp.concatenate([p.astype(F32) for p in split(v, 2)] + [none, none], axis=1).astype(BF16)
        return jnp.where(c_end == 0, 1.0, 0.0)

    def spread(first_head, width, parts):
        r, c = iota((128, 256), 0), iota((128, 256), 1)
        hit = ((r & 31) == first_head + c // width) & (r < 32 * parts)
        return jnp.where(hit, 1.0, 0.0).astype(BF16)

    def scaled(c):
        cols = pl.ds(pl.multiple_of(256 * c, 256), 256)
        oh = spread(4 * c, 64, 2)
        a = (dy[:, cols].astype(F32) * dot(ent2[...], oh)).astype(BF16)
        dys[:, cols] = a
        dyst[cols, :] = a.T
        b = (x[:, cols].astype(F32) * dot(end2[...], oh)).astype(BF16)
        xs[:, cols] = b
        xst[cols, :] = b.T
        m = dot(mid2[...], oh)
        p = (x[0:256, cols].astype(F32) * m[0:256]).astype(BF16)
        q = (dy[256:512, cols].astype(F32) * m[256:512]).astype(BF16)
        xe[:, cols] = p
        de[:, cols] = q
        dg10[...] += dot(q, p, 1, 1)

    def weights(r, hp, b, e):
        rb = r[256 * b : 256 * b + 256, 128 * e : 128 * e + 128]
        rt = runt[pl.ds(2 * hp + e, 1), 256 * b : 256 * b + 256]
        return jnp.concatenate([rb, rb], axis=1) - rt

    def one_head(v, e):
        return jnp.where((iota(v.shape, 1) // 64) == e, v, jnp.zeros_like(v))

    def dgram_pair(hp):
        r = dot(run3[...], spread(2 * hp, 128, 3))
        cols = pl.ds(pl.multiple_of(128 * hp, 128), 128)
        for b in (0, 1):
            rs = slice(256 * b, 256 * b + 256)
            dyp, xp = dy[rs, cols], x[rs, cols]
            total = dgd[b]
            for e in (0, 1):
                s = dot(dyp, one_head(xp, e), 1, 1)
                total += s * jnp.exp(jnp.minimum(weights(r, hp, b, e), 0.0))
            dgd[b] = total
        tail = jnp.exp(r[504:512, :])
        dtile[hp, 0:1, :] = tail[7:8, 0:128] * whole
        dtile[hp, 1:2, :] = tail[7:8, 128:256] * whole

    def send_decays():
        drecv[i] = dtile[i]

        def one(d):
            q = lax.rem(i + d, 16)
            remote(dtile.at[q], drecv.at[i], tsend.at[4, q], trecv.at[4, i], (q, j)).start()

        loop(1, 16, one)

    for half in (0, 1):
        send(half, "a", -1, 0, None, 1)
        send(half, "a", 1, 0, None, -1)
    for half in (0, 1):
        out_b(half, 0)
    acc[...] = jnp.zeros_like(acc)
    dg10[...] = jnp.zeros_like(dg10)
    dgd[...] = jnp.zeros_like(dgd)
    dtile[...] = jnp.zeros_like(dtile)
    whole = tables()
    loads[0].wait()
    loads[1].wait()
    for half in (0, 1):
        got(half, "a", -1, 0, None)
        send(half, "a", 2, 0, 0, 1)
        got(half, "a", 1, 0, None)
        send(half, "a", 2, 0, 1, -1)
    for half in (0, 1):
        out_b(half, -1)
        out_b(half, 1)
    loads[2].wait()
    loads[3].wait()
    mul([(0, 0)])
    loop(0, 4, dgram_pair)
    for half in (0, 1):
        fwd_b(half, 0)
    mul([(-1, 0), (1, 0)])
    for half in (0, 1):
        got(half, "a", 2, 0, 0)
        got(half, "a", 2, 0, 1)
        out_b(half, 2)
    loop(4, 8, dgram_pair)
    mul([(0, -1), (0, 1), (2, 0)])
    for half in (0, 1):
        fwd_b(half, -1)
        fwd_b(half, 1)
    loop(8, 16, dgram_pair)
    send_decays()
    mul([(-1, -1), (-1, 1), (1, -1), (1, 1)])
    for half in (0, 1):
        fwd_b(half, 2)
    loop(0, 8, scaled)
    dgb[0:256, 0:256] = (dgd[0] * msk[0:256, 0:256]).astype(BF16)
    dgb[256:512, 256:512] = (dgd[1] * msk[256:512, 256:512]).astype(BF16)
    dgb[256:512, 0:256] = (dg10[...] * msk[256:512, 0:256]).astype(BF16)
    dgb[0:256, 256:512] = jnp.zeros((256, 256), BF16)
    mul([(2, -1), (2, 1)])
    for da in (0, -1, 1, 2):
        for half in (0, 1):
            got(half, "b", da, 2, 0)
            got(half, "b", da, 2, 1)
        mul([(da, 2)])
    bc[...] = acc[...].astype(BF16)

    def pair_rows(q):
        return pl.ds(pl.multiple_of(128 * q, 128), 128)

    def states(kind, left, cols, out, into):
        def one(d):
            q = lax.rem(i + d, 16)
            out[q] = dot(left[pair_rows(q), :], bc[:, cols]).astype(BF16)
            remote(out.at[q], into.at[i], tsend.at[kind, q], trecv.at[kind, i], (q, j)).start()

        loop(1, 16, one)
        into[i] = dot(left[pair_rows(i), :], bc[:, cols]).astype(BF16)

    def wait_in(kind, into):
        def one(d):
            k = lax.rem(i + d, 16)
            remote(into.at[k], into.at[k], tsend.at[kind, k], trecv.at[kind, k], (k, j)).wait_recv()

        loop(1, 16, one)

    def wait_out(kind, src):
        def one(d):
            k = lax.rem(i + d, 16)
            remote(src.at[k], src.at[k], tsend.at[kind, k], trecv.at[kind, k], (k, j)).wait_send()

        loop(1, 16, one)

    def scan(kind, into, out, back, backward):
        def one(n, state):
            k = 15 - n if backward else n
            out[k] = state.astype(BF16)
            d = drecv[k]
            d0 = jnp.concatenate([d[0:1, :], d[0:1, :]], axis=1)
            d1 = jnp.concatenate([d[1:2, :], d[1:2, :]], axis=1)
            new = into[k].astype(F32)
            return jnp.concatenate([state[0:64] * d0 + new[0:64], state[64:128] * d1 + new[64:128]], axis=0)

        lax.fori_loop(0, 16, one, jnp.zeros((128, 256), F32))

        def ship(d):
            k = lax.rem(i + d, 16)
            remote(out.at[k], back.at[i], tsend.at[kind, k], trecv.at[kind, i], (k, j)).start()

        loop(1, 16, ship)
        back[i] = out[i]

    def intra_pair(hp):
        r = dot(run3[...], spread(2 * hp, 128, 3))
        cols = pl.ds(pl.multiple_of(128 * hp, 128), 128)
        for b in (0, 1):
            rs = slice(256 * b, 256 * b + 256)
            dyp, xp = dy[rs, cols], x[rs, cols]
            ya = jnp.zeros((256, 128), F32)
            da = jnp.zeros((256, 128), F32)
            for e in (0, 1):
                diff = weights(r, hp, b, e)
                mix = (gd[b] * jnp.exp(jnp.minimum(diff, 0.0))).astype(BF16)
                ya += dot(mix, one_head(xp, e))
                mixt = (gdt[b] * jnp.exp(jnp.minimum(-diff, 0.0))).astype(BF16)
                da += dot(mixt, one_head(dyp, e))
            yacc[rs, cols] = ya
            dxacc[rs, cols] = da

    def across(c):
        cols = pl.ds(pl.multiple_of(256 * c, 256), 256)
        m = dot(mid2[...], spread(4 * c, 64, 2))
        yacc[256:512, cols] += m[256:512] * dot(g10[...], xe[:, cols])
        dxacc[0:256, cols] += m[0:256] * dot(g10t[...], de[:, cols])

    states(0, xst, slice(0, 256), ssend, frecv)
    states(1, dyst, slice(256, 512), gsend, grecv)
    b_map, c_map = bc[:, 0:256], bc[:, 256:512]
    row = cnt[0:1, :]
    for b in (0, 1):
        rs = slice(256 * b, 256 * b + 256)
        gd[b] = dot(c_map[rs], b_map[rs], 1, 1) * msk[rs, rs]
        gdt[b] = dot(b_map[rs], c_map[rs], 1, 1) * msk[rs, rs].T
    g10[...] = (dot(c_map[256:512], b_map[0:256], 1, 1) * msk[256:512, 0:256]).astype(BF16)
    g10t[...] = (dot(b_map[0:256], c_map[256:512], 1, 1) * msk[256:512, 0:256].T).astype(BF16)
    acc[:, 0:256] = dot(dgb[...], c_map, 0, 0)
    acc[:, 256:512] = dot(dgb[...], b_map)
    loop(0, 6, intra_pair)
    wait_in(4, drecv)
    wait_in(0, frecv)
    wait_out(0, ssend)
    scan(2, frecv, ssend, sin, False)
    loop(6, 10, intra_pair)
    wait_in(1, grecv)
    wait_out(1, gsend)
    scan(3, grecv, gsend, rsum, True)
    loop(10, 16, intra_pair)
    loop(0, 8, across)
    wait_in(2, sin)
    acc[:, 256:512] += sum(dot(dys[:, 128 * q : 128 * q + 128], sin[q]) for q in range(16))
    wait_in(3, rsum)
    acc[:, 0:256] += sum(dot(xs[:, 128 * q : 128 * q + 128], rsum[q]) for q in range(16))
    bc2 = acc[...].T.astype(BF16)
    dgb[...] = bc2
    for c in sent:
        c.wait_send()

    top[...] = jnp.zeros_like(top)

    def block(k):
        cols = pl.ds(pl.multiple_of(512 * k, 512), 512)
        p = dot(dgb[...], hbuf[:, cols])
        top[...] = jnp.maximum(top[...], jnp.max(jnp.abs(p).reshape(64, 8, 512), axis=0))
        wbuf[k] = p.astype(BF16)

    loop(0, 16, block)
    largest = jnp.max(top[...])
    box[0] = jnp.full((8, 128), largest, F32)

    def spread_max(kind, count, dev):
        base = 16 * kind

        def ship(d):
            remote(box.at[0], box.at[base + d], msend.at[base + d], mrecv.at[base + d], dev(d)).start()

        def wait(d):
            remote(box.at[0], box.at[base + d], msend.at[base + d], mrecv.at[base + d], dev(d)).wait()

        loop(1, count, ship)
        loop(1, count, wait)
        best = box[0]
        for d in range(1, count):
            best = jnp.maximum(best, box[base + d])
        return best

    box[0] = spread_max(0, 16, lambda d: (lax.rem(i + d, 16), j))
    best = spread_max(1, 8, lambda d: (i, lax.rem(j + d, 8)))
    guess = jnp.ceil(jnp.log2(best)).astype(jnp.int32)
    guess = jnp.where(power_of_two(guess) < best, guess + 1, guess)
    guess = jnp.where(power_of_two(guess - 1) >= best, guess - 1, guess)
    exp_out[...] = guess.astype(F32)
    scale = jnp.max(power_of_two(20 - guess))

    def part_of(n):
        return lax.rem(6 - n // 2, 4), lax.rem(n, 2)

    def half_rows(half, at, size):
        return pl.ds(pl.multiple_of(256 * half + at, 128), size)

    def quant(k, rs):
        return jnp.floor(wbuf[k, rs, :].astype(F32) * scale + 0.5)

    def msg(n, t, src, dst, axis, sign, half):
        return remote(src, dst, rsend.at[n, t], rrecv.at[n, t], device(half, axis, sign))

    def stage0(n):
        da, half = part_of(n)
        k = owner(half, da, 2)
        rs = half_rows(half, 0, 256)
        wbuf[k, rs, :] = quant(k, rs).astype(BF16)
        msg(n, 0, wbuf.at[k, half_rows(half, 0, 128), :], s1.at[n, 0], "b", 1, half).start()
        msg(n, 1, wbuf.at[k, half_rows(half, 128, 128), :], s1.at[n, 1], "b", -1, half).start()

    def stage1(n):
        da, half = part_of(n)
        for t, sign in ((0, 1), (1, -1)):
            k = owner(half, da, sign)
            with_sum = half_rows(half, 128 * t, 128)
            alone = half_rows(half, 128 - 128 * t, 128)
            wbuf[k, alone, :] = quant(k, alone).astype(BF16)
            own = quant(k, with_sum)
            msg(n, t, s1.at[n, t], s1.at[n, t], "b", 1, half).wait_recv()
            wbuf[k, with_sum, :] = (own + s1[n, t].astype(F32)).astype(BF16)
            msg(n, 2 + t, wbuf.at[k, half_rows(half, 0, 256), :], f1.at[n, t], "b", sign, half).start()

    def total1(n):
        da, half = part_of(n)
        rs = half_rows(half, 0, 256)
        k = owner(half, da, 0)
        own = quant(k, rs)
        for t in (0, 1):
            msg(n, 2 + t, f1.at[n, t], f1.at[n, t], "b", 1, half).wait_recv()
        return k, rs, own + f1[n, 0].astype(F32) + f1[n, 1].astype(F32)

    def stage2(n):
        k, rs, total = total1(n)
        wbuf[k, rs, :] = total.astype(BF16)

    def finish_y(c):
        cols = pl.ds(pl.multiple_of(256 * c, 256), 256)
        oh = spread(4 * c, 64, 2)
        c_map, b_map = bc[:, 256:512], bc[:, 0:256]
        for t in (0, 1):
            at = pl.ds(pl.multiple_of(256 * c + 128 * t, 128), 128)
            hs = slice(128 * t, 128 * t + 128)
            carry = dot(c_map, sin[2 * c + t], 1, 1) * dot(ent2[...], oh[:, hs])
            hbuf[:, at] = (yacc[:, at] + carry).astype(BF16)
            carry = dot(b_map, rsum[2 * c + t], 1, 1) * dot(end2[...], oh[:, hs])
            hbuf[:, pl.ds(pl.multiple_of(2048 + 256 * c + 128 * t, 128), 128)] = (dxacc[:, at] + carry).astype(BF16)

    loop(0, 8, stage0)
    loop(0, 8, finish_y)
    ends = [
        pltpu.make_async_copy(hbuf.at[:, 0:2048], y_out, lsem.at[0]),
        pltpu.make_async_copy(hbuf.at[:, 2048:4096], dx_out, lsem.at[1]),
    ]
    for c in ends:
        c.start()
    loop(0, 8, stage1)
    loop(0, 2, stage2)

    def stage3(half):
        k = owner(half, 2, 0)
        msg(8 + half, 0, wbuf.at[k, half_rows(half, 0, 128), :], s2.at[half, 0], "a", 1, half).start()
        msg(8 + half, 1, wbuf.at[k, half_rows(half, 128, 128), :], s2.at[half, 1], "a", -1, half).start()

    loop(0, 2, stage3)
    loop(2, 4, stage2)
    loop(6, 8, stage2)

    def stage4(half):
        for t, sign in ((0, 1), (1, -1)):
            k = owner(half, sign, 0)
            rs = half_rows(half, 128 * t, 128)
            msg(8 + half, t, s2.at[half, t], s2.at[half, t], "a", 1, half).wait_recv()
            wbuf[k, rs, :] = (wbuf[k, rs, :].astype(F32) + s2[half, t].astype(F32)).astype(BF16)
            msg(8 + half, 2 + t, wbuf.at[k, half_rows(half, 0, 256), :], f2.at[half, t], "a", sign, half).start()

    loop(0, 2, stage4)

    def stage5(n):
        _, rs, total = total1(n)
        acc[rs, :] = total

    loop(4, 6, stage5)
    for half in (0, 1):
        for t in (0, 1):
            msg(8 + half, 2 + t, f2.at[half, t], f2.at[half, t], "a", 1, half).wait_recv()
        rs = slice(256 * half, 256 * half + 256)
        total = acc[rs, :] + f2[half, 0].astype(F32) + f2[half, 1].astype(F32)
        gm_out[:, rs] = (total * 2.0 ** -20).T

    for kind, src in ((2, ssend), (3, gsend), (4, dtile)):
        wait_out(kind, src)

    def left(n):
        for t in (0, 1):
            msg(n, t, s1.at[0, 0], s1.at[0, 0], "b", 1, 0).wait_send()
            msg(n, 2 + t, f1.at[0, 0], f1.at[0, 0], "b", 1, 0).wait_send()

    loop(0, 10, left)
    for c in ends:
        c.wait()


def mixer(lengths, hidden, w, x, log_decay, dy):
    n = len(PLAN)
    vm = pltpu.VMEM
    anyw = pl.BlockSpec(memory_space=pl.ANY)
    vspec = pl.BlockSpec(memory_space=pltpu.VMEM)
    scratch = [
        vm((512, 8192), BF16), vm((16, 512, 512), BF16), vm((512, 512), F32), vm((512, 512), BF16),
        vm((512, 2048), BF16), vm((512, 2048), BF16), vm((512, 2048), BF16), vm((512, 2048), BF16),
        vm((2048, 512), BF16), vm((2048, 512), BF16), vm((256, 2048), BF16), vm((256, 2048), BF16),
        vm((512, 2048), F32), vm((512, 2048), F32),
        vm((512, 128), BF16), vm((128, 512), F32), vm((512, 128), BF16), vm((512, 128), BF16), vm((512, 128), BF16),
        vm((8, 512), F32), vm((512, 512), F32), vm((2, 256, 256), F32), vm((256, 256), F32), vm((512, 512), BF16),
        vm((2, 256, 256), F32), vm((2, 256, 256), F32), vm((256, 256), BF16), vm((256, 256), BF16),
        vm((16, 128, 256), BF16), vm((16, 128, 256), BF16), vm((16, 128, 256), BF16), vm((16, 128, 256), BF16),
        vm((16, 128, 256), BF16), vm((16, 128, 256), BF16),
        vm((16, 8, 128), F32), vm((16, 8, 128), F32),
        vm((8, 2, 128, 512), BF16), vm((8, 2, 256, 512), BF16), vm((2, 2, 128, 512), BF16), vm((2, 2, 256, 512), BF16),
        vm((8, 512), F32), vm((32, 8, 128), F32),
        pltpu.SemaphoreType.DMA((4,)), pltpu.SemaphoreType.DMA((2, n)), pltpu.SemaphoreType.DMA((2, n)),
        pltpu.SemaphoreType.DMA((5, 16)), pltpu.SemaphoreType.DMA((5, 16)),
        pltpu.SemaphoreType.DMA((10, 4)), pltpu.SemaphoreType.DMA((10, 4)),
        pltpu.SemaphoreType.DMA((32,)), pltpu.SemaphoreType.DMA((32,)),
    ]
    y, dx, gm, ex = pl.pallas_call(
        kernel,
        out_shape=(
            jax.ShapeDtypeStruct((512, 2048), BF16), jax.ShapeDtypeStruct((512, 2048), BF16),
            jax.ShapeDtypeStruct((512, 512), F32), jax.ShapeDtypeStruct((8, 128), F32),
        ),
        in_specs=[pl.BlockSpec(memory_space=pltpu.SMEM), vspec, anyw, anyw, anyw, anyw],
        out_specs=(anyw, anyw, vspec, vspec),
        scratch_shapes=scratch,
        compiler_params=pltpu.CompilerParams(collective_id=0, has_side_effects=True, vmem_limit_bytes=63 * MB),
        name="mixer",
    )(lengths, log_decay, hidden, w, x, dy)
    return y, dx, gm, ex[0, 0]


def solution(mesh):
    in_specs = (P(), P("seq", None), P("seq", "mp"), P("seq", "mp"), P("seq", "mp"), P("seq", "mp"))
    out_specs = (P("seq", "mp"), P("seq", "mp"), P("seq", "mp"), P())
    return jax.shard_map(mixer, mesh=mesh, in_specs=in_specs, out_specs=out_specs, check_vma=False)
```

```python
import functools
import jax
import jax.numpy as jnp
from jax import lax
from jax.experimental import pallas as pl
from jax.experimental.pallas import tpu as pltpu
from jax.sharding import PartitionSpec as P

MESH = pl.DeviceIdType.MESH
MB = 1 << 20
F32, BF16 = jnp.float32, jnp.bfloat16


def dot(a, b, ca=1, cb=0):
    return lax.dot_general(a, b, (((ca,), (cb,)), ((), ())), preferred_element_type=F32)


def iota(shape, dim):
    return lax.broadcasted_iota(jnp.int32, shape, dim)


def loop(low, high, body):
    def one(n, carry):
        body(n)
        return carry

    lax.fori_loop(low, high, one, 0)


def gather_plan():
    plan = {}
    for da in (0, 1, -1, 2):
        if da:
            for q in (0, 1) if abs(da) == 2 else (None,):
                plan[("a", da, 0, q)] = len(plan)
        for db in (1, -1):
            plan[("b", da, db, None)] = len(plan)
        for q in (0, 1):
            plan[("b", da, 2, q)] = len(plan)
    return plan


PLAN = gather_plan()


def power_of_two(n):
    size = jnp.abs(n)
    up, down = jnp.ones(n.shape, F32), jnp.ones(n.shape, F32)
    for b in range(7):
        bit = ((size >> b) & 1) == 1
        up = jnp.where(bit, up * (2.0 ** (1 << b)), up)
        down = jnp.where(bit, down * (2.0 ** -(1 << b)), down)
    return jnp.where(n >= 0, up, down)


def kernel(
    lens, logd, hid, w, xin, dyin,
    y_out, dx_out, gm_out, exp_out,
    ldv, hbuf, wbuf, acc, bc, x, dy, xs, dys, xst, dyst, xe, de, yacc, dxacc,
    run3, runt, ent2, end2, mid2, cnt, msk, dgd, dg10, dgb, gd, gdt, g10, g10t,
    ssend, gsend, frecv, grecv, sin, rsum, dtile, drecv,
    s1, f1, s2, f2, top, box,
    lsem, asend, arecv, tsend, trecv, rsend, rrecv, msend, mrecv,
):
    i = lax.axis_index("seq")
    j = lax.axis_index("mp")
    px, py = i // 4, lax.rem(i, 4)

    def owner(half, da, db):
        dx = half * da + (1 - half) * db
        dyy = half * db + (1 - half) * da
        return lax.rem(px + dx + 4, 4) * 4 + lax.rem(py + dyy + 4, 4)

    def device(half, axis, sign):
        return (owner(half, sign, 0) if axis == "a" else owner(half, 0, sign), j)

    def remote(src, dst, send_sem, recv_sem, dev):
        return pltpu.make_async_remote_copy(
            src_ref=src, dst_ref=dst, send_sem=send_sem, recv_sem=recv_sem,
            device_id=dev, device_id_type=MESH,
        )

    own = [
        (w.at[256 * h : 256 * h + 256, 256 * p : 256 * p + 256], wbuf.at[i, p, h]) for p in (0, 1) for h in (0, 1)
    ]
    loads = [
        pltpu.make_async_copy(src, dst, lsem.at[n])
        for n, (src, dst) in enumerate(own + [(logd, ldv), (xin, x), (dyin, dy), (hid, hbuf)])
    ]
    for c in loads:
        c.start()
    barrier = pltpu.get_barrier_semaphore()
    for d in range(1, 16):
        pl.semaphore_signal(barrier, inc=1, device_id=(lax.rem(i + d, 16), j), device_id_type=MESH)
    for d in range(1, 8):
        pl.semaphore_signal(barrier, inc=1, device_id=(i, lax.rem(j + d, 8)), device_id_type=MESH)
    pl.semaphore_wait(barrier, 22)

    def rows(q):
        return pl.ds(0, 256) if q is None else pl.ds(128 * q, 128)

    sent = []

    def send(part, half, axis, da, db, q, sign):
        m = PLAN[(axis, da, db, q)]
        if axis == "a":
            oa, ob = (da + sign if abs(da) == 1 else -sign), 0
        else:
            oa, ob = da, (0 if abs(db) == 1 else -sign)
        k = owner(half, oa, ob)
        piece = wbuf.at[k, part, half, rows(q), :]
        c = remote(
            piece, piece,
            asend.at[part, half, m], arecv.at[part, half, m], device(half, axis, sign),
        )
        c.start()
        sent.append(c)

    def got(part, half, axis, da, db, q):
        m = PLAN[(axis, da, db, q)]
        ref = wbuf.at[owner(half, da, db), part, half, rows(q), :]
        remote(ref, ref, asend.at[part, half, m], arecv.at[part, half, m], device(half, axis, 1)).wait_recv()

    def out_b(part, half, da):
        send(part, half, "b", da, -1, None, 1)
        send(part, half, "b", da, 1, None, -1)

    def fwd_b(part, das):
        for da in das:
            for half in (0, 1):
                got(part, half, "b", da, -1, None)
                send(part, half, "b", da, 2, 0, 1)
                got(part, half, "b", da, 1, None)
                send(part, half, "b", da, 2, 1, -1)

    def step0(part):
        for half in (0, 1):
            send(part, half, "a", -1, 0, None, 1)
            send(part, half, "a", 1, 0, None, -1)
        for half in (0, 1):
            out_b(part, half, 0)

    def step1(part):
        for half in (0, 1):
            got(part, half, "a", -1, 0, None)
            send(part, half, "a", 2, 0, 0, 1)
            got(part, half, "a", 1, 0, None)
            send(part, half, "a", 2, 0, 1, -1)
        for half in (0, 1):
            out_b(part, half, -1)
            out_b(part, half, 1)

    def step3(part):
        for half in (0, 1):
            got(part, half, "a", 2, 0, 0)
            got(part, half, "a", 2, 0, 1)
            out_b(part, half, 2)

    def last(part, das):
        for da in das:
            for half in (0, 1):
                got(part, half, "b", da, 2, 0)
                got(part, half, "b", da, 2, 1)

    def mul(part, pairs):
        def one(n):
            half, r = lax.rem(n, 2), n // 2
            da = sum(jnp.where(r == t, p[0], 0) for t, p in enumerate(pairs))
            db = sum(jnp.where(r == t, p[1], 0) for t, p in enumerate(pairs))
            k = owner(half, da, db)
            off = pl.multiple_of(half * 256, 256)
            cols = pl.ds(pl.multiple_of(k * 512 + off, 256), 256)
            out = pl.ds(256 * part, 256)
            acc[:, out] += dot(hbuf[:, cols], wbuf[k, part, half])

        loop(0, 2 * len(pairs), one)

    def tables():
        tri = (iota((512, 512), 0) >= iota((512, 512), 1)).astype(F32).astype(BF16)

        def split(v, parts):
            out = []
            for _ in range(parts):
                top_part = v.astype(BF16)
                out.append(top_part)
                v = v - top_part.astype(F32)
            return out

        run = sum(dot(tri, p, 1, 1) for p in split(ldv[...], 3))
        none = jnp.zeros((512, 32), F32)
        run3[...] = jnp.concatenate([p.astype(F32) for p in split(run, 3)] + [none], axis=1).astype(BF16)
        runt[...] = jnp.concatenate([run, none, none, none], axis=1).T

        first = i * 512
        begin = jnp.int32(0)
        t_col, t_row = iota((512, 128), 0), iota((8, 512), 1)
        c_col, c_row = jnp.zeros((512, 128), jnp.int32), jnp.zeros((8, 512), jnp.int32)
        c_mid, c_end = jnp.int32(0), jnp.int32(0)
        for d in range(8):
            at = begin - first
            inside = jnp.where(at >= 0, 1, 0)
            c_col += jnp.where(t_col >= at, inside, 0)
            c_row += jnp.where(t_row >= at, inside, 0)
            c_mid += jnp.where(at <= 255, inside, 0)
            c_end += jnp.where(at <= 511, inside, 0)
            begin = begin + lens[d]
        cnt[0:8, :] = c_row.astype(F32)
        col, row = c_col[:, 0:1], c_row[0:1, :]
        same = jnp.where(col == row, 1.0, 0.0)
        msk[...] = jnp.where(iota((512, 512), 0) >= iota((512, 512), 1), same, 0.0)
        seg = c_col[:, 0:32]
        ent = jnp.where(seg == 0, jnp.exp(run), 0.0)
        end = jnp.where(seg == c_end, jnp.exp(jnp.minimum(run[511:512, :] - run, 0.0)), 0.0)
        mid = jnp.where(seg == c_mid, jnp.exp(-jnp.abs(run - run[255:256, :])), 0.0)
        for ref, v in ((ent2, ent), (end2, end), (mid2, mid)):
            ref[...] = jnp.concatenate([p.astype(F32) for p in split(v, 2)] + [none, none], axis=1).astype(BF16)
        return jnp.where(c_end == 0, 1.0, 0.0)

    def spread(first_head, width, parts):
        r, c = iota((128, 256), 0), iota((128, 256), 1)
        hit = ((r & 31) == first_head + c // width) & (r < 32 * parts)
        return jnp.where(hit, 1.0, 0.0).astype(BF16)

    def scaled(c):
        cols = pl.ds(pl.multiple_of(256 * c, 256), 256)
        oh = spread(4 * c, 64, 2)
        a = (dy[:, cols].astype(F32) * dot(ent2[...], oh)).astype(BF16)
        dys[:, cols] = a
        dyst[cols, :] = a.T
        b = (x[:, cols].astype(F32) * dot(end2[...], oh)).astype(BF16)
        xs[:, cols] = b
        xst[cols, :] = b.T
        m = dot(mid2[...], oh)
        p = (x[0:256, cols].astype(F32) * m[0:256]).astype(BF16)
        q = (dy[256:512, cols].astype(F32) * m[256:512]).astype(BF16)
        xe[:, cols] = p
        de[:, cols] = q
        dg10[...] += dot(q, p, 1, 1)

    def weights(r, hp, b, e):
        rb = r[256 * b : 256 * b + 256, 128 * e : 128 * e + 128]
        rt = runt[pl.ds(2 * hp + e, 1), 256 * b : 256 * b + 256]
        return jnp.concatenate([rb, rb], axis=1) - rt

    def one_head(v, e):
        return jnp.where((iota(v.shape, 1) // 64) == e, v, jnp.zeros_like(v))

    def dgram_pair(hp):
        r = dot(run3[...], spread(2 * hp, 128, 3))
        cols = pl.ds(pl.multiple_of(128 * hp, 128), 128)
        for b in (0, 1):
            rs = slice(256 * b, 256 * b + 256)
            dyp, xp = dy[rs, cols], x[rs, cols]
            total = dgd[b]
            for e in (0, 1):
                s = dot(dyp, one_head(xp, e), 1, 1)
                total += s * jnp.exp(jnp.minimum(weights(r, hp, b, e), 0.0))
            dgd[b] = total
        tail = jnp.exp(r[504:512, :])
        dtile[hp, 0:1, :] = tail[7:8, 0:128] * whole
        dtile[hp, 1:2, :] = tail[7:8, 128:256] * whole

    def send_decays():
        drecv[i] = dtile[i]

        def one(d):
            q = lax.rem(i + d, 16)
            remote(dtile.at[q], drecv.at[i], tsend.at[4, q], trecv.at[4, i], (q, j)).start()

        loop(1, 16, one)

    def pair_rows(q):
        return pl.ds(pl.multiple_of(128 * q, 128), 128)

    def states(kind, left, cols, out, into):
        def one(d):
            q = lax.rem(i + d, 16)
            out[q] = dot(left[pair_rows(q), :], bc[:, cols]).astype(BF16)
            remote(out.at[q], into.at[i], tsend.at[kind, q], trecv.at[kind, i], (q, j)).start()

        loop(1, 16, one)
        into[i] = dot(left[pair_rows(i), :], bc[:, cols]).astype(BF16)

    def wait_in(kind, into):
        def one(d):
            k = lax.rem(i + d, 16)
            ref = into.at[pair_rows(k), :] if kind in (2, 3) else into.at[k]
            remote(ref, ref, tsend.at[kind, k], trecv.at[kind, k], (k, j)).wait_recv()

        loop(1, 16, one)

    def wait_out(kind, src):
        def one(d):
            k = lax.rem(i + d, 16)
            remote(src.at[k], src.at[k], tsend.at[kind, k], trecv.at[kind, k], (k, j)).wait_send()

        loop(1, 16, one)

    def scan(kind, into, out, back, backward):
        def one(n, state):
            k = 15 - n if backward else n
            out[k] = state.astype(BF16)
            d = drecv[k]
            d0 = jnp.concatenate([d[0:1, :], d[0:1, :]], axis=1)
            d1 = jnp.concatenate([d[1:2, :], d[1:2, :]], axis=1)
            new = into[k].astype(F32)
            return jnp.concatenate([state[0:64] * d0 + new[0:64], state[64:128] * d1 + new[64:128]], axis=0)

        lax.fori_loop(0, 16, one, jnp.zeros((128, 256), F32))

        def ship(d):
            k = lax.rem(i + d, 16)
            remote(out.at[k], back.at[pair_rows(i), :], tsend.at[kind, k], trecv.at[kind, i], (k, j)).start()

        loop(1, 16, ship)
        back[pair_rows(i), :] = out[i]

    def intra_pair(hp):
        r = dot(run3[...], spread(2 * hp, 128, 3))
        cols = pl.ds(pl.multiple_of(128 * hp, 128), 128)
        for b in (0, 1):
            rs = slice(256 * b, 256 * b + 256)
            dyp, xp = dy[rs, cols], x[rs, cols]
            ya = jnp.zeros((256, 128), F32)
            da = jnp.zeros((256, 128), F32)
            for e in (0, 1):
                diff = weights(r, hp, b, e)
                mix = (gd[b] * jnp.exp(jnp.minimum(diff, 0.0))).astype(BF16)
                ya += dot(mix, one_head(xp, e))
                mixt = (gdt[b] * jnp.exp(jnp.minimum(-diff, 0.0))).astype(BF16)
                da += dot(mixt, one_head(dyp, e))
            yacc[rs, cols] = ya
            dxacc[rs, cols] = da

    def across(c):
        cols = pl.ds(pl.multiple_of(256 * c, 256), 256)
        m = dot(mid2[...], spread(4 * c, 64, 2))
        yacc[256:512, cols] += m[256:512] * dot(g10[...], xe[:, cols])
        dxacc[0:256, cols] += m[0:256] * dot(g10t[...], de[:, cols])

    for c in loads[0:4]:
        c.wait()
    step0(0)
    acc[...] = jnp.zeros_like(acc)
    dg10[...] = jnp.zeros_like(dg10)
    dgd[...] = jnp.zeros_like(dgd)
    dtile[...] = jnp.zeros_like(dtile)
    loads[4].wait()
    whole = tables()
    loads[5].wait()
    loads[6].wait()
    step1(0)
    step0(1)
    loads[7].wait()
    mul(0, [(0, 0), (-1, 0), (1, 0)])
    fwd_b(0, (0,))
    loop(0, 4, dgram_pair)
    step3(0)
    step1(1)
    mul(0, [(0, -1), (0, 1), (2, 0)])
    mul(1, [(0, 0), (-1, 0), (1, 0)])
    fwd_b(0, (-1, 1))
    fwd_b(1, (0,))
    loop(4, 10, dgram_pair)
    fwd_b(0, (2,))
    step3(1)
    loop(0, 4, scaled)
    mul(0, [(-1, -1), (-1, 1), (1, -1), (1, 1)])
    fwd_b(1, (-1, 1))
    mul(1, [(0, -1), (0, 1), (2, 0)])
    loop(4, 8, scaled)
    last(0, (0, -1, 1))
    mul(0, [(2, -1), (2, 1), (0, 2), (-1, 2), (1, 2)])
    fwd_b(1, (2,))
    last(0, (2,))
    mul(0, [(2, 2)])
    bc[:, 0:256] = acc[:, 0:256].astype(BF16)
    states(0, xst, slice(0, 256), ssend, frecv)
    mul(1, [(-1, -1), (-1, 1), (1, -1), (1, 1), (2, -1), (2, 1)])
    loop(10, 16, dgram_pair)
    send_decays()
    last(1, (0, -1, 1))
    mul(1, [(0, 2), (-1, 2), (1, 2)])
    last(1, (2,))
    mul(1, [(2, 2)])
    bc[:, 256:512] = acc[:, 256:512].astype(BF16)
    states(1, dyst, slice(256, 512), gsend, grecv)
    dgb[0:256, 0:256] = (dgd[0] * msk[0:256, 0:256]).astype(BF16)
    dgb[256:512, 256:512] = (dgd[1] * msk[256:512, 256:512]).astype(BF16)
    dgb[256:512, 0:256] = (dg10[...] * msk[256:512, 0:256]).astype(BF16)
    dgb[0:256, 256:512] = jnp.zeros((256, 256), BF16)
    b_map, c_map = bc[:, 0:256], bc[:, 256:512]
    row = cnt[0:1, :]
    for b in (0, 1):
        rs = slice(256 * b, 256 * b + 256)
        gd[b] = dot(c_map[rs], b_map[rs], 1, 1) * msk[rs, rs]
        gdt[b] = dot(b_map[rs], c_map[rs], 1, 1) * msk[rs, rs].T
    g10[...] = (dot(c_map[256:512], b_map[0:256], 1, 1) * msk[256:512, 0:256]).astype(BF16)
    g10t[...] = (dot(b_map[0:256], c_map[256:512], 1, 1) * msk[256:512, 0:256].T).astype(BF16)
    acc[:, 0:256] = dot(dgb[...], c_map, 0, 0)
    acc[:, 256:512] = dot(dgb[...], b_map)
    loop(0, 6, intra_pair)
    wait_in(4, drecv)
    wait_in(0, frecv)
    wait_out(0, ssend)
    scan(2, frecv, ssend, sin, False)
    loop(6, 10, intra_pair)
    wait_in(1, grecv)
    wait_out(1, gsend)
    scan(3, grecv, gsend, rsum, True)
    loop(10, 16, intra_pair)
    loop(0, 8, across)
    def part_of(n):
        g = n // 4
        return 1 - lax.rem(n // 2, 2), lax.rem(2 + 3 * g + 3 * (g // 2) + 2 * (g // 3), 4), lax.rem(n, 2)

    def at_rows(part, at, size):
        return pl.ds(pl.multiple_of(256 * part + at, 128), size)

    def at_cols(half):
        return pl.ds(pl.multiple_of(256 * half, 256), 256)

    def floored(v):
        return jnp.floor(v.astype(F32) * scale + 0.5)

    def msg(n, t, src, dst, axis, sign, half):
        return remote(src, dst, rsend.at[n, t], rrecv.at[n, t], device(half, axis, sign))

    def stage0(n):
        part, da, half = part_of(n)
        k = owner(half, da, 2)
        for t, sign in ((0, 1), (1, -1)):
            src = wbuf.at[k, part, half, 128 * t : 128 * t + 128, :]
            msg(n, t, src, s1.at[n, t], "b", sign, half).start()

    def block_of(part):
        def block(k):
            cols = pl.ds(pl.multiple_of(512 * k, 512), 512)
            p = dot(dgb[256 * part : 256 * part + 256, :], hbuf[:, cols])
            top[...] = jnp.maximum(top[...], jnp.max(jnp.abs(p).reshape(32, 8, 512), axis=0))
            wbuf[k, part, 0] = p[:, 0:256].astype(BF16)
            wbuf[k, part, 1] = p[:, 256:512].astype(BF16)

        loop(0, 16, block)

    top[...] = jnp.zeros_like(top)
    for c in sent:
        c.wait_send()
    wait_in(2, sin)
    acc[:, 256:512] += dot(dys[...], sin[...])
    dgb[256:512, :] = acc[:, 256:512].T.astype(BF16)
    block_of(1)
    wait_in(3, rsum)
    loop(0, 8, lambda m: stage0(4 * (m // 2) + lax.rem(m, 2)))
    acc[:, 0:256] += dot(xs[...], rsum[...])
    dgb[0:256, :] = acc[:, 0:256].T.astype(BF16)
    block_of(0)
    loop(0, 8, lambda m: stage0(4 * (m // 2) + 2 + lax.rem(m, 2)))
    def finish_y(c):
        cols = pl.ds(pl.multiple_of(256 * c, 256), 256)
        oh = spread(4 * c, 64, 2)
        c_map, b_map = bc[:, 256:512], bc[:, 0:256]
        for t in (0, 1):
            at = pl.ds(pl.multiple_of(256 * c + 128 * t, 128), 128)
            hs = slice(128 * t, 128 * t + 128)
            carry = dot(c_map, sin[at, :], 1, 1) * dot(ent2[...], oh[:, hs])
            hbuf[:, at] = (yacc[:, at] + carry).astype(BF16)
            carry = dot(b_map, rsum[at, :], 1, 1) * dot(end2[...], oh[:, hs])
            hbuf[:, pl.ds(pl.multiple_of(2048 + 256 * c + 128 * t, 128), 128)] = (dxacc[:, at] + carry).astype(BF16)

    def ship_max(kind, count, dev):
        base = 16 * kind
        loop(1, count, lambda d: remote(
            box.at[base], box.at[base + d], msend.at[base + d], mrecv.at[base + d], dev(d)).start())

    def best_of(kind, count, dev):
        base = 16 * kind
        loop(1, count, lambda d: remote(
            box.at[base], box.at[base + d], msend.at[base + d], mrecv.at[base + d], dev(d)).wait())
        best = box[base]
        for d in range(1, count):
            best = jnp.maximum(best, box[base + d])
        return best

    along_seq = (16, lambda d: (lax.rem(i + d, 16), j))
    along_mp = (8, lambda d: (i, lax.rem(j + d, 8)))
    most = top[:, 0:128]
    for c in range(1, 4):
        most = jnp.maximum(most, top[:, 128 * c : 128 * c + 128])
    box[0] = most
    ship_max(0, *along_seq)
    loop(0, 4, finish_y)
    box[16] = best_of(0, *along_seq)
    ship_max(1, *along_mp)
    loop(4, 8, finish_y)
    best = jnp.full((8, 128), jnp.max(best_of(1, *along_mp)), F32)
    guess = jnp.ceil(jnp.log2(best)).astype(jnp.int32)
    guess = jnp.where(power_of_two(guess) < best, guess + 1, guess)
    guess = jnp.where(power_of_two(guess - 1) >= best, guess - 1, guess)
    exp_out[...] = guess.astype(F32)
    scale = jnp.max(power_of_two(20 - guess))

    def stage1(n):
        part, da, half = part_of(n)
        for t, sign in ((0, 1), (1, -1)):
            piece = wbuf.at[owner(half, da, sign), part, half]
            with_sum = slice(128 * t, 128 * t + 128)
            alone = slice(128 - 128 * t, 256 - 128 * t)
            piece[alone, :] = floored(piece[alone, :]).astype(BF16)
            own = floored(piece[with_sum, :])
            msg(n, t, s1.at[n, t], s1.at[n, t], "b", 1, half).wait_recv()
            piece[with_sum, :] = (own + floored(s1[n, t])).astype(BF16)
            msg(n, 2 + t, piece, f1.at[n, t], "b", sign, half).start()

    def total1(n):
        part, da, half = part_of(n)
        k = owner(half, da, 0)
        own = floored(wbuf[k, part, half])
        for t in (0, 1):
            msg(n, 2 + t, f1.at[n, t], f1.at[n, t], "b", 1, half).wait_recv()
        return k, part, half, own + f1[n, 0].astype(F32) + f1[n, 1].astype(F32)

    def stage2(n):
        k, part, half, total = total1(n)
        wbuf[k, part, half] = total.astype(BF16)

    def stage3(s):
        part, half = 1 - s // 2, lax.rem(s, 2)
        k = owner(half, 2, 0)
        for t, sign in ((0, 1), (1, -1)):
            src = wbuf.at[k, part, half, 128 * t : 128 * t + 128, :]
            msg(16 + s, t, src, s2.at[s, t], "a", sign, half).start()

    def stage4(s):
        part, half = 1 - s // 2, lax.rem(s, 2)
        for t, sign in ((0, 1), (1, -1)):
            piece = wbuf.at[owner(half, sign, 0), part, half]
            rs = slice(128 * t, 128 * t + 128)
            msg(16 + s, t, s2.at[s, t], s2.at[s, t], "a", 1, half).wait_recv()
            piece[rs, :] = (piece[rs, :].astype(F32) + s2[s, t].astype(F32)).astype(BF16)
            msg(16 + s, 2 + t, piece, f2.at[s, t], "a", sign, half).start()

    def stage5(n):
        _, part, half, total = total1(n)
        acc[at_rows(part, 0, 256), at_cols(half)] = total

    def stage6(s):
        part, half = 1 - s // 2, lax.rem(s, 2)
        for t in (0, 1):
            msg(16 + s, 2 + t, f2.at[s, t], f2.at[s, t], "a", 1, half).wait_recv()
        rs, cs = at_rows(part, 0, 256), at_cols(half)
        gm_out[rs, cs] = acc[rs, cs] + f2[s, 0].astype(F32) + f2[s, 1].astype(F32)

    ends = [
        pltpu.make_async_copy(hbuf.at[:, 0:2048], y_out, lsem.at[0]),
        pltpu.make_async_copy(hbuf.at[:, 2048:4096], dx_out, lsem.at[1]),
    ]
    for c in ends:
        c.start()
    loop(0, 8, stage1)
    loop(0, 4, stage2)
    loop(0, 4, stage3)
    loop(8, 12, stage1)
    loop(4, 8, stage2)
    loop(12, 16, stage1)
    loop(8, 12, stage2)
    loop(0, 4, stage4)
    loop(12, 16, stage5)
    loop(0, 4, stage6)

    for kind, src in ((2, ssend), (3, gsend), (4, dtile)):
        wait_out(kind, src)

    def left(n):
        for t in (0, 1):
            msg(n, t, s1.at[0, 0], s1.at[0, 0], "b", 1, 0).wait_send()
            msg(n, 2 + t, f1.at[0, 0], f1.at[0, 0], "b", 1, 0).wait_send()

    loop(0, 20, left)
    for c in ends:
        c.wait()


def finish(y_in, dx_in, gm_in, exp_in, y_out, dx_out, gm_out, exp_out):
    y_out[...] = y_in[...]
    dx_out[...] = dx_in[...]
    gm_out[...] = (gm_in[...] * 2.0 ** -20).T
    exp_out[...] = exp_in[0:1, 0:1]


def mixer(lengths, hidden, w, x, log_decay, dy):
    n = len(PLAN)
    vm = pltpu.VMEM
    anyw = pl.BlockSpec(memory_space=pl.ANY)
    vspec = pl.BlockSpec(memory_space=pltpu.VMEM)
    scratch = [
        vm((32, 512), F32), vm((512, 8192), BF16), vm((16, 2, 2, 256, 256), BF16), vm((512, 512), F32), vm((512, 512), BF16),
        vm((512, 2048), BF16), vm((512, 2048), BF16), vm((512, 2048), BF16), vm((512, 2048), BF16),
        vm((2048, 512), BF16), vm((2048, 512), BF16), vm((256, 2048), BF16), vm((256, 2048), BF16),
        vm((512, 2048), F32), vm((512, 2048), F32),
        vm((512, 128), BF16), vm((128, 512), F32), vm((512, 128), BF16), vm((512, 128), BF16), vm((512, 128), BF16),
        vm((8, 512), F32), vm((512, 512), F32), vm((2, 256, 256), F32), vm((256, 256), F32), vm((512, 512), BF16),
        vm((2, 256, 256), F32), vm((2, 256, 256), F32), vm((256, 256), BF16), vm((256, 256), BF16),
        vm((16, 128, 256), BF16), vm((16, 128, 256), BF16), vm((16, 128, 256), BF16), vm((16, 128, 256), BF16),
        vm((2048, 256), BF16), vm((2048, 256), BF16),
        vm((16, 8, 128), F32), vm((16, 8, 128), F32),
        vm((16, 2, 128, 256), BF16), vm((16, 2, 256, 256), BF16), vm((4, 2, 128, 256), BF16), vm((4, 2, 256, 256), BF16),
        vm((8, 512), F32), vm((32, 8, 128), F32),
        pltpu.SemaphoreType.DMA((8,)), pltpu.SemaphoreType.DMA((2, 2, n)), pltpu.SemaphoreType.DMA((2, 2, n)),
        pltpu.SemaphoreType.DMA((5, 16)), pltpu.SemaphoreType.DMA((5, 16)),
        pltpu.SemaphoreType.DMA((20, 4)), pltpu.SemaphoreType.DMA((20, 4)),
        pltpu.SemaphoreType.DMA((32,)), pltpu.SemaphoreType.DMA((32,)),
    ]
    y, dx, gm, ex = pl.pallas_call(
        kernel,
        out_shape=(
            jax.ShapeDtypeStruct((512, 2048), BF16), jax.ShapeDtypeStruct((512, 2048), BF16),
            jax.ShapeDtypeStruct((512, 512), F32), jax.ShapeDtypeStruct((8, 128), F32),
        ),
        in_specs=[pl.BlockSpec(memory_space=pltpu.SMEM), anyw, anyw, anyw, anyw, anyw],
        out_specs=(anyw, anyw, vspec, vspec),
        scratch_shapes=scratch,
        compiler_params=pltpu.CompilerParams(collective_id=0, has_side_effects=True, vmem_limit_bytes=63 * MB),
        name="mixer",
    )(lengths, log_decay.T, hidden, w, x, dy)
    y, dx, gm, ex = pl.pallas_call(
        finish,
        out_shape=(
            jax.ShapeDtypeStruct((512, 2048), BF16), jax.ShapeDtypeStruct((512, 2048), BF16),
            jax.ShapeDtypeStruct((512, 512), F32), jax.ShapeDtypeStruct((1, 1), F32),
        ),
        grid=(4,),
        in_specs=[
            pl.BlockSpec((128, 2048), lambda g: (g, 0)), pl.BlockSpec((128, 2048), lambda g: (g, 0)),
            pl.BlockSpec((512, 128), lambda g: (0, g)), pl.BlockSpec((8, 128), lambda g: (0, 0)),
        ],
        out_specs=(
            pl.BlockSpec((128, 2048), lambda g: (g, 0)), pl.BlockSpec((128, 2048), lambda g: (g, 0)),
            pl.BlockSpec((128, 512), lambda g: (g, 0)), pl.BlockSpec((1, 1), lambda g: (0, 0)),
        ),
        name="finish",
    )(y, dx, gm, ex)
    return y, dx, gm, ex.reshape(())


def solution(mesh):
    in_specs = (P(), P("seq", None), P("seq", "mp"), P("seq", "mp"), P("seq", "mp"), P("seq", "mp"))
    out_specs = (P("seq", "mp"), P("seq", "mp"), P("seq", "mp"), P())
    return jax.shard_map(mixer, mesh=mesh, in_specs=in_specs, out_specs=out_specs, check_vma=False)
```

```python
import functools
import jax
import jax.numpy as jnp
from jax import lax
from jax.experimental import pallas as pl
from jax.experimental.pallas import tpu as pltpu
from jax.sharding import PartitionSpec as P

MESH = pl.DeviceIdType.MESH
MB = 1 << 20
F32, BF16 = jnp.float32, jnp.bfloat16


def dot(a, b, ca=1, cb=0):
    return lax.dot_general(a, b, (((ca,), (cb,)), ((), ())), preferred_element_type=F32)


def iota(shape, dim):
    return lax.broadcasted_iota(jnp.int32, shape, dim)


def loop(low, high, body):
    def one(n, carry):
        body(n)
        return carry

    lax.fori_loop(low, high, one, 0)


def gather_plan():
    plan = {}
    for da in (0, 1, -1, 2):
        if da:
            for q in (0, 1) if abs(da) == 2 else (None,):
                plan[("a", da, 0, q)] = len(plan)
        for db in (1, -1):
            plan[("b", da, db, None)] = len(plan)
        for q in (0, 1):
            plan[("b", da, 2, q)] = len(plan)
    return plan


PLAN = gather_plan()

NEAR = [(0, 1), (1, 0), (0, 3), (3, 0), (1, 1), (3, 3), (1, 3), (3, 1), (0, 2), (2, 0), (1, 2), (2, 1), (3, 2), (2, 3), (2, 2)]


def power_of_two(n):
    size = jnp.abs(n)
    up, down = jnp.ones(n.shape, F32), jnp.ones(n.shape, F32)
    for b in range(7):
        bit = ((size >> b) & 1) == 1
        up = jnp.where(bit, up * (2.0 ** (1 << b)), up)
        down = jnp.where(bit, down * (2.0 ** -(1 << b)), down)
    return jnp.where(n >= 0, up, down)


def kernel(
    lens, logd, hid, w, xin, dyin,
    y_out, dx_out, gm_out, exp_out,
    ldv, hbuf, wbuf, acc, bc, x, dy, xs, dys, xst, dyst, xe, de, yacc, dxacc,
    run3, runt, ent2, end2, mid2, cnt, msk, dgd, dg10, dgb, gd, gdt, g10, g10t,
    ssend, gsend, frecv, grecv, sin, rsum, dtile, drecv,
    s1, f1, s2, f2, top, box,
    lsem, asend, arecv, tsend, trecv, rsend, rrecv, msend, mrecv,
):
    i = lax.axis_index("seq")
    j = lax.axis_index("mp")
    px, py = i // 4, lax.rem(i, 4)

    def owner(half, da, db):
        dx = half * da + (1 - half) * db
        dyy = half * db + (1 - half) * da
        return lax.rem(px + dx + 4, 4) * 4 + lax.rem(py + dyy + 4, 4)

    def device(half, axis, sign):
        return (owner(half, sign, 0) if axis == "a" else owner(half, 0, sign), j)

    def remote(src, dst, send_sem, recv_sem, dev):
        return pltpu.make_async_remote_copy(
            src_ref=src, dst_ref=dst, send_sem=send_sem, recv_sem=recv_sem,
            device_id=dev, device_id_type=MESH,
        )

    own = [
        (w.at[256 * h : 256 * h + 256, 256 * p : 256 * p + 256], wbuf.at[i, p, h]) for p in (0, 1) for h in (0, 1)
    ]
    loads = [
        pltpu.make_async_copy(src, dst, lsem.at[n])
        for n, (src, dst) in enumerate(own + [(logd, ldv), (xin, x), (dyin, dy), (hid, hbuf)])
    ]
    for c in loads:
        c.start()
    barrier = pltpu.get_barrier_semaphore()
    for d in range(1, 16):
        pl.semaphore_signal(barrier, inc=1, device_id=(lax.rem(i + d, 16), j), device_id_type=MESH)
    for d in range(1, 8):
        pl.semaphore_signal(barrier, inc=1, device_id=(i, lax.rem(j + d, 8)), device_id_type=MESH)
    pl.semaphore_wait(barrier, 22)

    def rows(q):
        return pl.ds(0, 256) if q is None else pl.ds(128 * q, 128)

    sent = []

    def send(part, half, axis, da, db, q, sign):
        m = PLAN[(axis, da, db, q)]
        if axis == "a":
            oa, ob = (da + sign if abs(da) == 1 else -sign), 0
        else:
            oa, ob = da, (0 if abs(db) == 1 else -sign)
        k = owner(half, oa, ob)
        piece = wbuf.at[k, part, half, rows(q), :]
        c = remote(
            piece, piece,
            asend.at[part, half, m], arecv.at[part, half, m], device(half, axis, sign),
        )
        c.start()
        sent.append(c)

    def got(part, half, axis, da, db, q):
        m = PLAN[(axis, da, db, q)]
        ref = wbuf.at[owner(half, da, db), part, half, rows(q), :]
        remote(ref, ref, asend.at[part, half, m], arecv.at[part, half, m], device(half, axis, 1)).wait_recv()

    def out_b(part, half, da):
        send(part, half, "b", da, -1, None, 1)
        send(part, half, "b", da, 1, None, -1)

    def fwd_b(part, das):
        for da in das:
            for half in (0, 1):
                got(part, half, "b", da, -1, None)
                send(part, half, "b", da, 2, 0, 1)
                got(part, half, "b", da, 1, None)
                send(part, half, "b", da, 2, 1, -1)

    def step0(part):
        for half in (0, 1):
            send(part, half, "a", -1, 0, None, 1)
            send(part, half, "a", 1, 0, None, -1)
        for half in (0, 1):
            out_b(part, half, 0)

    def step1(part):
        for half in (0, 1):
            got(part, half, "a", -1, 0, None)
            send(part, half, "a", 2, 0, 0, 1)
            got(part, half, "a", 1, 0, None)
            send(part, half, "a", 2, 0, 1, -1)
        for half in (0, 1):
            out_b(part, half, -1)
            out_b(part, half, 1)

    def step3(part):
        for half in (0, 1):
            got(part, half, "a", 2, 0, 0)
            got(part, half, "a", 2, 0, 1)
            out_b(part, half, 2)

    def last(part, das):
        for da in das:
            for half in (0, 1):
                got(part, half, "b", da, 2, 0)
                got(part, half, "b", da, 2, 1)

    def mul(part, pairs):
        def one(n):
            half, r = lax.rem(n, 2), n // 2
            da = sum(jnp.where(r == t, p[0], 0) for t, p in enumerate(pairs))
            db = sum(jnp.where(r == t, p[1], 0) for t, p in enumerate(pairs))
            k = owner(half, da, db)
            off = pl.multiple_of(half * 256, 256)
            cols = pl.ds(pl.multiple_of(k * 512 + off, 256), 256)
            out = pl.ds(256 * part, 256)
            acc[:, out] += dot(hbuf[:, cols], wbuf[k, part, half])

        loop(0, 2 * len(pairs), one)

    def tables():
        tri = (iota((512, 512), 0) >= iota((512, 512), 1)).astype(F32).astype(BF16)

        def split(v, parts):
            out = []
            for _ in range(parts):
                top_part = v.astype(BF16)
                out.append(top_part)
                v = v - top_part.astype(F32)
            return out

        run = sum(dot(tri, p, 1, 1) for p in split(ldv[...], 3))
        none = jnp.zeros((512, 32), F32)
        run3[...] = jnp.concatenate([p.astype(F32) for p in split(run, 3)] + [none], axis=1).astype(BF16)
        runt[...] = jnp.concatenate([run, none, none, none], axis=1).T

        first = i * 512
        begin = jnp.int32(0)
        t_col, t_row = iota((512, 128), 0), iota((8, 512), 1)
        c_col, c_row = jnp.zeros((512, 128), jnp.int32), jnp.zeros((8, 512), jnp.int32)
        c_mid, c_end = jnp.int32(0), jnp.int32(0)
        for d in range(8):
            at = begin - first
            inside = jnp.where(at >= 0, 1, 0)
            c_col += jnp.where(t_col >= at, inside, 0)
            c_row += jnp.where(t_row >= at, inside, 0)
            c_mid += jnp.where(at <= 255, inside, 0)
            c_end += jnp.where(at <= 511, inside, 0)
            begin = begin + lens[d]
        cnt[0:8, :] = c_row.astype(F32)
        col, row = c_col[:, 0:1], c_row[0:1, :]
        same = jnp.where(col == row, 1.0, 0.0)
        msk[...] = jnp.where(iota((512, 512), 0) >= iota((512, 512), 1), same, 0.0)
        seg = c_col[:, 0:32]
        ent = jnp.where(seg == 0, jnp.exp(run), 0.0)
        end = jnp.where(seg == c_end, jnp.exp(jnp.minimum(run[511:512, :] - run, 0.0)), 0.0)
        mid = jnp.where(seg == c_mid, jnp.exp(-jnp.abs(run - run[255:256, :])), 0.0)
        for ref, v in ((ent2, ent), (end2, end), (mid2, mid)):
            ref[...] = jnp.concatenate([p.astype(F32) for p in split(v, 2)] + [none, none], axis=1).astype(BF16)
        return jnp.where(c_end == 0, 1.0, 0.0)

    def spread(first_head, width, parts):
        r, c = iota((128, 256), 0), iota((128, 256), 1)
        hit = ((r & 31) == first_head + c // width) & (r < 32 * parts)
        return jnp.where(hit, 1.0, 0.0).astype(BF16)

    def scaled(c):
        cols = pl.ds(pl.multiple_of(256 * c, 256), 256)
        oh = spread(4 * c, 64, 2)
        a = (dy[:, cols].astype(F32) * dot(ent2[...], oh)).astype(BF16)
        dys[:, cols] = a
        dyst[cols, :] = a.T
        b = (x[:, cols].astype(F32) * dot(end2[...], oh)).astype(BF16)
        xs[:, cols] = b
        xst[cols, :] = b.T
        m = dot(mid2[...], oh)
        p = (x[0:256, cols].astype(F32) * m[0:256]).astype(BF16)
        q = (dy[256:512, cols].astype(F32) * m[256:512]).astype(BF16)
        xe[:, cols] = p
        de[:, cols] = q
        dg10[...] += dot(q, p, 1, 1)

    def weights(r, hp, b, e):
        rb = r[256 * b : 256 * b + 256, 128 * e : 128 * e + 128]
        rt = runt[pl.ds(2 * hp + e, 1), 256 * b : 256 * b + 256]
        return jnp.concatenate([rb, rb], axis=1) - rt

    def one_head(v, e):
        return jnp.where((iota(v.shape, 1) // 64) == e, v, jnp.zeros_like(v))

    def dgram_pair(hp):
        r = dot(run3[...], spread(2 * hp, 128, 3))
        cols = pl.ds(pl.multiple_of(128 * hp, 128), 128)
        for b in (0, 1):
            rs = slice(256 * b, 256 * b + 256)
            dyp, xp = dy[rs, cols], x[rs, cols]
            total = dgd[b]
            for e in (0, 1):
                s = dot(dyp, one_head(xp, e), 1, 1)
                total += s * jnp.exp(jnp.minimum(weights(r, hp, b, e), 0.0))
            dgd[b] = total
        tail = jnp.exp(r[504:512, :])
        dtile[hp, 0:1, :] = tail[7:8, 0:128] * whole
        dtile[hp, 1:2, :] = tail[7:8, 128:256] * whole

    def send_decays():
        drecv[i] = dtile[i]

        def one(d):
            q = lax.rem(i + d, 16)
            remote(dtile.at[q], drecv.at[i], tsend.at[4, q], trecv.at[4, i], (q, j)).start()

        loop(1, 16, one)

    def pair_rows(q):
        return pl.ds(pl.multiple_of(128 * q, 128), 128)

    def states(kind, left, cols, out, into, peers):
        for dx, dyy in peers:
            q = owner(1, dx, dyy)
            out[q] = dot(left[pair_rows(q), :], bc[:, cols]).astype(BF16)
            remote(out.at[q], into.at[i], tsend.at[kind, q], trecv.at[kind, i], (q, j)).start()
        if peers[0] == NEAR[0]:
            into[i] = dot(left[pair_rows(i), :], bc[:, cols]).astype(BF16)

    def wait_in(kind, into):
        def one(d):
            k = lax.rem(i + d, 16)
            ref = into.at[pair_rows(k), :] if kind in (2, 3) else into.at[k]
            remote(ref, ref, tsend.at[kind, k], trecv.at[kind, k], (k, j)).wait_recv()

        loop(1, 16, one)

    def wait_out(kind, src):
        def one(d):
            k = lax.rem(i + d, 16)
            remote(src.at[k], src.at[k], tsend.at[kind, k], trecv.at[kind, k], (k, j)).wait_send()

        loop(1, 16, one)

    def scan(kind, into, out, back, backward):
        def one(n, state):
            k = 15 - n if backward else n
            out[k] = state.astype(BF16)
            d = drecv[k]
            d0 = jnp.concatenate([d[0:1, :], d[0:1, :]], axis=1)
            d1 = jnp.concatenate([d[1:2, :], d[1:2, :]], axis=1)
            new = into[k].astype(F32)
            return jnp.concatenate([state[0:64] * d0 + new[0:64], state[64:128] * d1 + new[64:128]], axis=0)

        lax.fori_loop(0, 16, one, jnp.zeros((128, 256), F32))

        for dx, dyy in NEAR:
            k = owner(1, dx, dyy)
            remote(out.at[k], back.at[pair_rows(i), :], tsend.at[kind, k], trecv.at[kind, i], (k, j)).start()
        back[pair_rows(i), :] = out[i]

    def intra_pair(hp):
        r = dot(run3[...], spread(2 * hp, 128, 3))
        cols = pl.ds(pl.multiple_of(128 * hp, 128), 128)
        for b in (0, 1):
            rs = slice(256 * b, 256 * b + 256)
            dyp, xp = dy[rs, cols], x[rs, cols]
            ya = jnp.zeros((256, 128), F32)
            da = jnp.zeros((256, 128), F32)
            for e in (0, 1):
                diff = weights(r, hp, b, e)
                mix = (gd[b] * jnp.exp(jnp.minimum(diff, 0.0))).astype(BF16)
                ya += dot(mix, one_head(xp, e))
                mixt = (gdt[b] * jnp.exp(jnp.minimum(-diff, 0.0))).astype(BF16)
                da += dot(mixt, one_head(dyp, e))
            yacc[rs, cols] = ya
            dxacc[rs, cols] = da

    def across(c):
        cols = pl.ds(pl.multiple_of(256 * c, 256), 256)
        m = dot(mid2[...], spread(4 * c, 64, 2))
        yacc[256:512, cols] += m[256:512] * dot(g10[...], xe[:, cols])
        dxacc[0:256, cols] += m[0:256] * dot(g10t[...], de[:, cols])

    for c in loads[0:4]:
        c.wait()
    step0(0)
    acc[...] = jnp.zeros_like(acc)
    dg10[...] = jnp.zeros_like(dg10)
    dgd[...] = jnp.zeros_like(dgd)
    dtile[...] = jnp.zeros_like(dtile)
    loads[4].wait()
    whole = tables()
    loads[5].wait()
    loads[6].wait()
    step1(0)
    step0(1)
    loads[7].wait()
    mul(0, [(0, 0), (-1, 0), (1, 0)])
    fwd_b(0, (0,))
    loop(0, 4, dgram_pair)
    step3(0)
    step1(1)
    mul(0, [(0, -1), (0, 1), (2, 0)])
    mul(1, [(0, 0), (-1, 0), (1, 0)])
    fwd_b(0, (-1, 1))
    fwd_b(1, (0,))
    loop(4, 10, dgram_pair)
    fwd_b(0, (2,))
    step3(1)
    loop(0, 4, scaled)
    mul(0, [(-1, -1), (-1, 1), (1, -1), (1, 1)])
    fwd_b(1, (-1, 1))
    mul(1, [(0, -1), (0, 1), (2, 0)])
    loop(4, 8, scaled)
    last(0, (0, -1, 1))
    mul(0, [(2, -1), (2, 1), (0, 2), (-1, 2), (1, 2)])
    fwd_b(1, (2,))
    last(0, (2,))
    mul(0, [(2, 2)])
    bc[:, 0:256] = acc[:, 0:256].astype(BF16)
    states(0, xst, slice(0, 256), ssend, frecv, NEAR)
    mul(1, [(-1, -1), (-1, 1), (1, -1), (1, 1), (2, -1), (2, 1)])
    loop(10, 16, dgram_pair)
    send_decays()
    last(1, (0, -1, 1))
    mul(1, [(0, 2), (-1, 2), (1, 2)])
    last(1, (2,))
    mul(1, [(2, 2)])
    bc[:, 256:512] = acc[:, 256:512].astype(BF16)
    states(1, dyst, slice(256, 512), gsend, grecv, NEAR[0:8])
    dgb[0:256, 0:256] = (dgd[0] * msk[0:256, 0:256]).astype(BF16)
    dgb[256:512, 256:512] = (dgd[1] * msk[256:512, 256:512]).astype(BF16)
    dgb[256:512, 0:256] = (dg10[...] * msk[256:512, 0:256]).astype(BF16)
    dgb[0:256, 256:512] = jnp.zeros((256, 256), BF16)
    b_map, c_map = bc[:, 0:256], bc[:, 256:512]
    row = cnt[0:1, :]
    for b in (0, 1):
        rs = slice(256 * b, 256 * b + 256)
        gd[b] = dot(c_map[rs], b_map[rs], 1, 1) * msk[rs, rs]
        gdt[b] = dot(b_map[rs], c_map[rs], 1, 1) * msk[rs, rs].T
    g10[...] = (dot(c_map[256:512], b_map[0:256], 1, 1) * msk[256:512, 0:256]).astype(BF16)
    g10t[...] = (dot(b_map[0:256], c_map[256:512], 1, 1) * msk[256:512, 0:256].T).astype(BF16)
    acc[:, 0:256] = dot(dgb[...], c_map, 0, 0)
    acc[:, 256:512] = dot(dgb[...], b_map)
    wait_in(4, drecv)
    wait_in(0, frecv)
    wait_out(0, ssend)
    scan(2, frecv, ssend, sin, False)
    states(1, dyst, slice(256, 512), gsend, grecv, NEAR[8:15])
    loop(0, 6, intra_pair)
    wait_in(1, grecv)
    wait_out(1, gsend)
    scan(3, grecv, gsend, rsum, True)
    loop(6, 10, intra_pair)
    def part_of(n):
        g = n // 4
        return 1 - lax.rem(n // 2, 2), lax.rem(2 + 3 * g + 3 * (g // 2) + 2 * (g // 3), 4), lax.rem(n, 2)

    def at_rows(part, at, size):
        return pl.ds(pl.multiple_of(256 * part + at, 128), size)

    def at_cols(half):
        return pl.ds(pl.multiple_of(256 * half, 256), 256)

    def floored(v):
        return jnp.floor(v.astype(F32) * scale + 0.5)

    def msg(n, t, src, dst, axis, sign, half):
        return remote(src, dst, rsend.at[n, t], rrecv.at[n, t], device(half, axis, sign))

    def stage0(n):
        part, da, half = part_of(n)
        k = owner(half, da, 2)
        for t, sign in ((0, 1), (1, -1)):
            src = wbuf.at[k, part, half, 128 * t : 128 * t + 128, :]
            msg(n, t, src, s1.at[n, t], "b", sign, half).start()

    def block_of(part):
        def block(k):
            cols = pl.ds(pl.multiple_of(512 * k, 512), 512)
            p = dot(dgb[256 * part : 256 * part + 256, :], hbuf[:, cols])
            top[...] = jnp.maximum(top[...], jnp.max(jnp.abs(p).reshape(32, 8, 512), axis=0))
            wbuf[k, part, 0] = p[:, 0:256].astype(BF16)
            wbuf[k, part, 1] = p[:, 256:512].astype(BF16)

        loop(0, 16, block)

    top[...] = jnp.zeros_like(top)
    for c in sent:
        c.wait_send()
    wait_in(2, sin)
    acc[:, 256:512] += dot(dys[...], sin[...])
    dgb[256:512, :] = acc[:, 256:512].T.astype(BF16)
    block_of(1)
    wait_in(3, rsum)
    loop(0, 8, lambda m: stage0(4 * (m // 2) + lax.rem(m, 2)))
    acc[:, 0:256] += dot(xs[...], rsum[...])
    dgb[0:256, :] = acc[:, 0:256].T.astype(BF16)
    block_of(0)
    def finish_y(c):
        cols = pl.ds(pl.multiple_of(256 * c, 256), 256)
        oh = spread(4 * c, 64, 2)
        c_map, b_map = bc[:, 256:512], bc[:, 0:256]
        for t in (0, 1):
            at = pl.ds(pl.multiple_of(256 * c + 128 * t, 128), 128)
            hs = slice(128 * t, 128 * t + 128)
            carry = dot(c_map, sin[at, :], 1, 1) * dot(ent2[...], oh[:, hs])
            hbuf[:, at] = (yacc[:, at] + carry).astype(BF16)
            carry = dot(b_map, rsum[at, :], 1, 1) * dot(end2[...], oh[:, hs])
            hbuf[:, pl.ds(pl.multiple_of(2048 + 256 * c + 128 * t, 128), 128)] = (dxacc[:, at] + carry).astype(BF16)

    def ship_max(kind, count, dev):
        base = 16 * kind
        loop(1, count, lambda d: remote(
            box.at[base], box.at[base + d], msend.at[base + d], mrecv.at[base + d], dev(d)).start())

    def best_of(kind, count, dev):
        base = 16 * kind
        loop(1, count, lambda d: remote(
            box.at[base], box.at[base + d], msend.at[base + d], mrecv.at[base + d], dev(d)).wait())
        best = box[base]
        for d in range(1, count):
            best = jnp.maximum(best, box[base + d])
        return best

    along_seq = (16, lambda d: (lax.rem(i + d, 16), j))
    along_mp = (8, lambda d: (i, lax.rem(j + d, 8)))
    most = top[:, 0:128]
    for c in range(1, 4):
        most = jnp.maximum(most, top[:, 128 * c : 128 * c + 128])
    box[0] = most
    ship_max(0, *along_seq)
    loop(0, 8, lambda m: stage0(4 * (m // 2) + 2 + lax.rem(m, 2)))
    loop(10, 13, intra_pair)
    box[16] = best_of(0, *along_seq)
    ship_max(1, *along_mp)
    loop(13, 16, intra_pair)
    best = jnp.full((8, 128), jnp.max(best_of(1, *along_mp)), F32)
    guess = jnp.ceil(jnp.log2(best)).astype(jnp.int32)
    guess = jnp.where(power_of_two(guess) < best, guess + 1, guess)
    guess = jnp.where(power_of_two(guess - 1) >= best, guess - 1, guess)
    exp_out[...] = guess.astype(F32)
    scale = jnp.max(power_of_two(20 - guess))

    def stage1(n):
        part, da, half = part_of(n)
        for t, sign in ((0, 1), (1, -1)):
            piece = wbuf.at[owner(half, da, sign), part, half]
            with_sum = slice(128 * t, 128 * t + 128)
            alone = slice(128 - 128 * t, 256 - 128 * t)
            piece[alone, :] = floored(piece[alone, :]).astype(BF16)
            own = floored(piece[with_sum, :])
            msg(n, t, s1.at[n, t], s1.at[n, t], "b", 1, half).wait_recv()
            piece[with_sum, :] = (own + floored(s1[n, t])).astype(BF16)
            msg(n, 2 + t, piece, f1.at[n, t], "b", sign, half).start()

    def total1(n):
        part, da, half = part_of(n)
        k = owner(half, da, 0)
        own = floored(wbuf[k, part, half])
        for t in (0, 1):
            msg(n, 2 + t, f1.at[n, t], f1.at[n, t], "b", 1, half).wait_recv()
        return k, part, half, own + f1[n, 0].astype(F32) + f1[n, 1].astype(F32)

    def stage2(n):
        k, part, half, total = total1(n)
        wbuf[k, part, half] = total.astype(BF16)

    def stage3(s):
        part, half = 1 - s // 2, lax.rem(s, 2)
        k = owner(half, 2, 0)
        for t, sign in ((0, 1), (1, -1)):
            src = wbuf.at[k, part, half, 128 * t : 128 * t + 128, :]
            msg(16 + s, t, src, s2.at[s, t], "a", sign, half).start()

    def stage4(s):
        part, half = 1 - s // 2, lax.rem(s, 2)
        for t, sign in ((0, 1), (1, -1)):
            piece = wbuf.at[owner(half, sign, 0), part, half]
            rs = slice(128 * t, 128 * t + 128)
            msg(16 + s, t, s2.at[s, t], s2.at[s, t], "a", 1, half).wait_recv()
            piece[rs, :] = (piece[rs, :].astype(F32) + s2[s, t].astype(F32)).astype(BF16)
            msg(16 + s, 2 + t, piece, f2.at[s, t], "a", sign, half).start()

    def stage5(n):
        _, part, half, total = total1(n)
        acc[at_rows(part, 0, 256), at_cols(half)] = total

    def stage6(s):
        part, half = 1 - s // 2, lax.rem(s, 2)
        for t in (0, 1):
            msg(16 + s, 2 + t, f2.at[s, t], f2.at[s, t], "a", 1, half).wait_recv()
        rs, cs = at_rows(part, 0, 256), at_cols(half)
        gm_out[rs, cs] = acc[rs, cs] + f2[s, 0].astype(F32) + f2[s, 1].astype(F32)

    loop(0, 8, stage1)
    loop(0, 8, across)
    loop(0, 4, stage2)
    loop(0, 4, stage3)
    loop(8, 12, stage1)
    loop(0, 4, finish_y)
    loop(4, 8, stage2)
    loop(12, 16, stage1)
    loop(4, 8, finish_y)
    ends = [
        pltpu.make_async_copy(hbuf.at[:, 0:2048], y_out, lsem.at[0]),
        pltpu.make_async_copy(hbuf.at[:, 2048:4096], dx_out, lsem.at[1]),
    ]
    for c in ends:
        c.start()
    loop(8, 12, stage2)
    loop(0, 4, stage4)
    loop(12, 16, stage5)
    loop(0, 4, stage6)

    for kind, src in ((2, ssend), (3, gsend), (4, dtile)):
        wait_out(kind, src)

    def left(n):
        for t in (0, 1):
            msg(n, t, s1.at[0, 0], s1.at[0, 0], "b", 1, 0).wait_send()
            msg(n, 2 + t, f1.at[0, 0], f1.at[0, 0], "b", 1, 0).wait_send()

    loop(0, 20, left)
    for c in ends:
        c.wait()


def finish(y_in, dx_in, gm_in, exp_in, y_out, dx_out, gm_out, exp_out, buf, gbuf, gout, sem, out_sem):
    pieces, size = 2, 256
    moves = []
    for a, (src, dst) in enumerate(((y_in, y_out), (dx_in, dx_out))):
        for p in range(pieces):
            rows = pl.ds(size * p, size)
            n = a * pieces + p
            moves.append((
                pltpu.make_async_copy(src.at[rows, :], buf.at[a, rows, :], sem.at[n]),
                pltpu.make_async_copy(buf.at[a, rows, :], dst.at[rows, :], out_sem.at[n]),
            ))
    g_in = pltpu.make_async_copy(gm_in, gbuf, sem.at[2 * pieces])
    g_out = pltpu.make_async_copy(gout, gm_out, out_sem.at[2 * pieces])
    g_in.start()
    for load, _ in moves:
        load.start()
    exp_out[...] = exp_in[0:1, 0:1]
    g_in.wait()
    gout[...] = (gbuf[...] * 2.0 ** -20).T
    g_out.start()
    for load, store in moves:
        load.wait()
        store.start()
    for _, store in moves:
        store.wait()
    g_out.wait()


def mixer(lengths, hidden, w, x, log_decay, dy):
    n = len(PLAN)
    vm = pltpu.VMEM
    anyw = pl.BlockSpec(memory_space=pl.ANY)
    vspec = pl.BlockSpec(memory_space=pltpu.VMEM)
    scratch = [
        vm((32, 512), F32), vm((512, 8192), BF16), vm((16, 2, 2, 256, 256), BF16), vm((512, 512), F32), vm((512, 512), BF16),
        vm((512, 2048), BF16), vm((512, 2048), BF16), vm((512, 2048), BF16), vm((512, 2048), BF16),
        vm((2048, 512), BF16), vm((2048, 512), BF16), vm((256, 2048), BF16), vm((256, 2048), BF16),
        vm((512, 2048), F32), vm((512, 2048), F32),
        vm((512, 128), BF16), vm((128, 512), F32), vm((512, 128), BF16), vm((512, 128), BF16), vm((512, 128), BF16),
        vm((8, 512), F32), vm((512, 512), F32), vm((2, 256, 256), F32), vm((256, 256), F32), vm((512, 512), BF16),
        vm((2, 256, 256), F32), vm((2, 256, 256), F32), vm((256, 256), BF16), vm((256, 256), BF16),
        vm((16, 128, 256), BF16), vm((16, 128, 256), BF16), vm((16, 128, 256), BF16), vm((16, 128, 256), BF16),
        vm((2048, 256), BF16), vm((2048, 256), BF16),
        vm((16, 8, 128), F32), vm((16, 8, 128), F32),
        vm((16, 2, 128, 256), BF16), vm((16, 2, 256, 256), BF16), vm((4, 2, 128, 256), BF16), vm((4, 2, 256, 256), BF16),
        vm((8, 512), F32), vm((32, 8, 128), F32),
        pltpu.SemaphoreType.DMA((8,)), pltpu.SemaphoreType.DMA((2, 2, n)), pltpu.SemaphoreType.DMA((2, 2, n)),
        pltpu.SemaphoreType.DMA((5, 16)), pltpu.SemaphoreType.DMA((5, 16)),
        pltpu.SemaphoreType.DMA((20, 4)), pltpu.SemaphoreType.DMA((20, 4)),
        pltpu.SemaphoreType.DMA((32,)), pltpu.SemaphoreType.DMA((32,)),
    ]
    y, dx, gm, ex = pl.pallas_call(
        kernel,
        out_shape=(
            jax.ShapeDtypeStruct((512, 2048), BF16), jax.ShapeDtypeStruct((512, 2048), BF16),
            jax.ShapeDtypeStruct((512, 512), F32), jax.ShapeDtypeStruct((8, 128), F32),
        ),
        in_specs=[pl.BlockSpec(memory_space=pltpu.SMEM), anyw, anyw, anyw, anyw, anyw],
        out_specs=(anyw, anyw, vspec, vspec),
        scratch_shapes=scratch,
        compiler_params=pltpu.CompilerParams(collective_id=0, has_side_effects=True, vmem_limit_bytes=63 * MB),
        name="mixer",
    )(lengths, log_decay.T, hidden, w, x, dy)
    y, dx, gm, ex = pl.pallas_call(
        finish,
        out_shape=(
            jax.ShapeDtypeStruct((512, 2048), BF16), jax.ShapeDtypeStruct((512, 2048), BF16),
            jax.ShapeDtypeStruct((512, 512), F32), jax.ShapeDtypeStruct((1, 1), F32),
        ),
        in_specs=[anyw, anyw, anyw, vspec],
        out_specs=(anyw, anyw, anyw, vspec),
        scratch_shapes=[
            vm((2, 512, 2048), BF16), vm((512, 512), F32), vm((512, 512), F32),
            pltpu.SemaphoreType.DMA((5,)), pltpu.SemaphoreType.DMA((5,)),
        ],
        compiler_params=pltpu.CompilerParams(vmem_limit_bytes=62 * MB),
        name="finish",
    )(y, dx, gm, ex)
    return y, dx, gm, ex.reshape(())


def solution(mesh):
    in_specs = (P(), P("seq", None), P("seq", "mp"), P("seq", "mp"), P("seq", "mp"), P("seq", "mp"))
    out_specs = (P("seq", "mp"), P("seq", "mp"), P("seq", "mp"), P())
    return jax.shard_map(mixer, mesh=mesh, in_specs=in_specs, out_specs=out_specs, check_vma=False)
```

```python
import functools
import jax
import jax.numpy as jnp
from jax import lax
from jax.experimental import pallas as pl
from jax.experimental.pallas import tpu as pltpu
from jax.sharding import PartitionSpec as P

MESH = pl.DeviceIdType.MESH
MB = 1 << 20
F32, BF16 = jnp.float32, jnp.bfloat16


def dot(a, b, ca=1, cb=0):
    return lax.dot_general(a, b, (((ca,), (cb,)), ((), ())), preferred_element_type=F32)


def iota(shape, dim):
    return lax.broadcasted_iota(jnp.int32, shape, dim)


def loop(low, high, body):
    def one(n, carry):
        body(n)
        return carry

    lax.fori_loop(low, high, one, 0)


def gather_plan():
    plan = {}
    for da in (0, 1, -1, 2):
        if da:
            for q in (0, 1) if abs(da) == 2 else (None,):
                plan[("a", da, 0, q)] = len(plan)
        for db in (1, -1):
            plan[("b", da, db, None)] = len(plan)
        for q in (0, 1):
            plan[("b", da, 2, q)] = len(plan)
    return plan


PLAN = gather_plan()

NEAR = [(0, 1), (1, 0), (0, 3), (3, 0), (1, 1), (3, 3), (1, 3), (3, 1), (0, 2), (2, 0), (1, 2), (2, 1), (3, 2), (2, 3), (2, 2)]


def power_of_two(n):
    size = jnp.abs(n)
    up, down = jnp.ones(n.shape, F32), jnp.ones(n.shape, F32)
    for b in range(7):
        bit = ((size >> b) & 1) == 1
        up = jnp.where(bit, up * (2.0 ** (1 << b)), up)
        down = jnp.where(bit, down * (2.0 ** -(1 << b)), down)
    return jnp.where(n >= 0, up, down)


def kernel(
    lens, logd, hid, w, xin, dyin,
    y_out, dx_out, gm_out, exp_out,
    ldv, hbuf, wbuf, acc, bc, x, dy, xs, dys, xst, dyst, xe, de, yacc, dxacc,
    run3, runt, ent2, end2, mid2, cnt, msk, dgd, dg10, dgb, gd, gdt, g10, g10t,
    ssend, gsend, frecv, grecv, sin, rsum, dtile, drecv,
    s1, f1, s2, f2, top, box,
    lsem, asend, arecv, tsend, trecv, rsend, rrecv, msend, mrecv,
):
    i = lax.axis_index("seq")
    j = lax.axis_index("mp")
    px, py = i // 4, lax.rem(i, 4)

    def owner(half, da, db):
        dx = half * da + (1 - half) * db
        dyy = half * db + (1 - half) * da
        return lax.rem(px + dx + 4, 4) * 4 + lax.rem(py + dyy + 4, 4)

    def device(half, axis, sign):
        return (owner(half, sign, 0) if axis == "a" else owner(half, 0, sign), j)

    def remote(src, dst, send_sem, recv_sem, dev):
        return pltpu.make_async_remote_copy(
            src_ref=src, dst_ref=dst, send_sem=send_sem, recv_sem=recv_sem,
            device_id=dev, device_id_type=MESH,
        )

    own = [
        (w.at[256 * h : 256 * h + 256, 256 * p : 256 * p + 256], wbuf.at[i, p, h]) for p in (0, 1) for h in (0, 1)
    ]
    loads = [
        pltpu.make_async_copy(src, dst, lsem.at[n])
        for n, (src, dst) in enumerate(own + [(logd, ldv), (xin, x), (dyin, dy), (hid, hbuf)])
    ]
    for c in loads:
        c.start()
    barrier = pltpu.get_barrier_semaphore()
    for d in range(1, 16):
        pl.semaphore_signal(barrier, inc=1, device_id=(lax.rem(i + d, 16), j), device_id_type=MESH)
    for d in range(1, 8):
        pl.semaphore_signal(barrier, inc=1, device_id=(i, lax.rem(j + d, 8)), device_id_type=MESH)
    pl.semaphore_wait(barrier, 22)

    def rows(q):
        return pl.ds(0, 256) if q is None else pl.ds(128 * q, 128)

    sent = []

    def send(part, half, axis, da, db, q, sign):
        m = PLAN[(axis, da, db, q)]
        if axis == "a":
            oa, ob = (da + sign if abs(da) == 1 else -sign), 0
        else:
            oa, ob = da, (0 if abs(db) == 1 else -sign)
        k = owner(half, oa, ob)
        piece = wbuf.at[k, part, half, rows(q), :]
        c = remote(
            piece, piece,
            asend.at[part, half, m], arecv.at[part, half, m], device(half, axis, sign),
        )
        c.start()
        sent.append(c)

    def got(part, half, axis, da, db, q):
        m = PLAN[(axis, da, db, q)]
        ref = wbuf.at[owner(half, da, db), part, half, rows(q), :]
        remote(ref, ref, asend.at[part, half, m], arecv.at[part, half, m], device(half, axis, 1)).wait_recv()

    def out_b(part, half, da):
        send(part, half, "b", da, -1, None, 1)
        send(part, half, "b", da, 1, None, -1)

    def fwd_b(part, das):
        for da in das:
            for half in (0, 1):
                got(part, half, "b", da, -1, None)
                send(part, half, "b", da, 2, 0, 1)
                got(part, half, "b", da, 1, None)
                send(part, half, "b", da, 2, 1, -1)

    def step0(part):
        for half in (0, 1):
            send(part, half, "a", -1, 0, None, 1)
            send(part, half, "a", 1, 0, None, -1)
        for half in (0, 1):
            out_b(part, half, 0)

    def step1(part):
        for half in (0, 1):
            got(part, half, "a", -1, 0, None)
            send(part, half, "a", 2, 0, 0, 1)
            got(part, half, "a", 1, 0, None)
            send(part, half, "a", 2, 0, 1, -1)
        for half in (0, 1):
            out_b(part, half, -1)
            out_b(part, half, 1)

    def step3(part):
        for half in (0, 1):
            got(part, half, "a", 2, 0, 0)
            got(part, half, "a", 2, 0, 1)
            out_b(part, half, 2)

    def last(part, das):
        for da in das:
            for half in (0, 1):
                got(part, half, "b", da, 2, 0)
                got(part, half, "b", da, 2, 1)

    def mul(part, pairs):
        def one(n):
            half, r = lax.rem(n, 2), n // 2
            da = sum(jnp.where(r == t, p[0], 0) for t, p in enumerate(pairs))
            db = sum(jnp.where(r == t, p[1], 0) for t, p in enumerate(pairs))
            k = owner(half, da, db)
            off = pl.multiple_of(half * 256, 256)
            cols = pl.ds(pl.multiple_of(k * 512 + off, 256), 256)
            out = pl.ds(256 * part, 256)
            acc[:, out] += dot(hbuf[:, cols], wbuf[k, part, half])

        loop(0, 2 * len(pairs), one)

    def tables():
        tri = (iota((512, 512), 0) >= iota((512, 512), 1)).astype(F32).astype(BF16)

        def split(v, parts):
            out = []
            for _ in range(parts):
                top_part = v.astype(BF16)
                out.append(top_part)
                v = v - top_part.astype(F32)
            return out

        run = sum(dot(tri, p, 1, 1) for p in split(ldv[...], 3))
        none = jnp.zeros((512, 32), F32)
        run3[...] = jnp.concatenate([p.astype(F32) for p in split(run, 3)] + [none], axis=1).astype(BF16)
        runt[...] = jnp.concatenate([run, none, none, none], axis=1).T

        first = i * 512
        begin = jnp.int32(0)
        t_col, t_row = iota((512, 128), 0), iota((8, 512), 1)
        c_col, c_row = jnp.zeros((512, 128), jnp.int32), jnp.zeros((8, 512), jnp.int32)
        c_mid, c_end = jnp.int32(0), jnp.int32(0)
        for d in range(8):
            at = begin - first
            inside = jnp.where(at >= 0, 1, 0)
            c_col += jnp.where(t_col >= at, inside, 0)
            c_row += jnp.where(t_row >= at, inside, 0)
            c_mid += jnp.where(at <= 255, inside, 0)
            c_end += jnp.where(at <= 511, inside, 0)
            begin = begin + lens[d]
        cnt[0:8, :] = c_row.astype(F32)
        col, row = c_col[:, 0:1], c_row[0:1, :]
        same = jnp.where(col == row, 1.0, 0.0)
        msk[...] = jnp.where(iota((512, 512), 0) >= iota((512, 512), 1), same, 0.0)
        seg = c_col[:, 0:32]
        ent = jnp.where(seg == 0, jnp.exp(run), 0.0)
        end = jnp.where(seg == c_end, jnp.exp(jnp.minimum(run[511:512, :] - run, 0.0)), 0.0)
        mid = jnp.where(seg == c_mid, jnp.exp(-jnp.abs(run - run[255:256, :])), 0.0)
        for ref, v in ((ent2, ent), (end2, end), (mid2, mid)):
            ref[...] = jnp.concatenate([p.astype(F32) for p in split(v, 2)] + [none, none], axis=1).astype(BF16)
        return jnp.where(c_end == 0, 1.0, 0.0)

    def spread(first_head, width, parts):
        r, c = iota((128, 256), 0), iota((128, 256), 1)
        hit = ((r & 31) == first_head + c // width) & (r < 32 * parts)
        return jnp.where(hit, 1.0, 0.0).astype(BF16)

    def scaled(c):
        cols = pl.ds(pl.multiple_of(256 * c, 256), 256)
        oh = spread(4 * c, 64, 2)
        a = (dy[:, cols].astype(F32) * dot(ent2[...], oh)).astype(BF16)
        dys[:, cols] = a
        dyst[cols, :] = a.T
        b = (x[:, cols].astype(F32) * dot(end2[...], oh)).astype(BF16)
        xs[:, cols] = b
        xst[cols, :] = b.T
        m = dot(mid2[...], oh)
        p = (x[0:256, cols].astype(F32) * m[0:256]).astype(BF16)
        q = (dy[256:512, cols].astype(F32) * m[256:512]).astype(BF16)
        xe[:, cols] = p
        de[:, cols] = q
        dg10[...] += dot(q, p, 1, 1)

    def weights(r, hp, b, e):
        rb = r[256 * b : 256 * b + 256, 128 * e : 128 * e + 128]
        rt = runt[pl.ds(2 * hp + e, 1), 256 * b : 256 * b + 256]
        return jnp.concatenate([rb, rb], axis=1) - rt

    def one_head(v, e):
        return jnp.where((iota(v.shape, 1) // 64) == e, v, jnp.zeros_like(v))

    def dgram_pair(hp):
        r = dot(run3[...], spread(2 * hp, 128, 3))
        cols = pl.ds(pl.multiple_of(128 * hp, 128), 128)
        for b in (0, 1):
            rs = slice(256 * b, 256 * b + 256)
            dyp, xp = dy[rs, cols], x[rs, cols]
            total = dgd[b]
            for e in (0, 1):
                s = dot(dyp, one_head(xp, e), 1, 1)
                total += s * jnp.exp(jnp.minimum(weights(r, hp, b, e), 0.0))
            dgd[b] = total
        tail = jnp.exp(r[504:512, :])
        dtile[hp, 0:1, :] = tail[7:8, 0:128] * whole
        dtile[hp, 1:2, :] = tail[7:8, 128:256] * whole

    def send_decays():
        drecv[i] = dtile[i]

        def one(d):
            q = lax.rem(i + d, 16)
            remote(dtile.at[q], drecv.at[i], tsend.at[4, q], trecv.at[4, i], (q, j)).start()

        loop(1, 16, one)

    def pair_rows(q):
        return pl.ds(pl.multiple_of(128 * q, 128), 128)

    def states(kind, left, cols, out, into, peers):
        for dx, dyy in peers:
            q = owner(1, dx, dyy)
            out[q] = dot(left[pair_rows(q), :], bc[:, cols]).astype(BF16)
            remote(out.at[q], into.at[i], tsend.at[kind, q], trecv.at[kind, i], (q, j)).start()
        if peers[0] == NEAR[0]:
            into[i] = dot(left[pair_rows(i), :], bc[:, cols]).astype(BF16)

    def wait_in(kind, into):
        def one(d):
            k = lax.rem(i + d, 16)
            ref = into.at[pair_rows(k), :] if kind in (2, 3) else into.at[k]
            remote(ref, ref, tsend.at[kind, k], trecv.at[kind, k], (k, j)).wait_recv()

        loop(1, 16, one)

    def wait_out(kind, src):
        def one(d):
            k = lax.rem(i + d, 16)
            remote(src.at[k], src.at[k], tsend.at[kind, k], trecv.at[kind, k], (k, j)).wait_send()

        loop(1, 16, one)

    def scan(kind, into, out, back, backward):
        def one(n, state):
            k = 15 - n if backward else n
            out[k] = state.astype(BF16)
            d = drecv[k]
            d0 = jnp.concatenate([d[0:1, :], d[0:1, :]], axis=1)
            d1 = jnp.concatenate([d[1:2, :], d[1:2, :]], axis=1)
            new = into[k].astype(F32)
            return jnp.concatenate([state[0:64] * d0 + new[0:64], state[64:128] * d1 + new[64:128]], axis=0)

        lax.fori_loop(0, 16, one, jnp.zeros((128, 256), F32))

        for dx, dyy in NEAR:
            k = owner(1, dx, dyy)
            remote(out.at[k], back.at[pair_rows(i), :], tsend.at[kind, k], trecv.at[kind, i], (k, j)).start()
        back[pair_rows(i), :] = out[i]

    def intra_pair(hp):
        r = dot(run3[...], spread(2 * hp, 128, 3))
        cols = pl.ds(pl.multiple_of(128 * hp, 128), 128)
        for b in (0, 1):
            rs = slice(256 * b, 256 * b + 256)
            dyp, xp = dy[rs, cols], x[rs, cols]
            ya = jnp.zeros((256, 128), F32)
            da = jnp.zeros((256, 128), F32)
            for e in (0, 1):
                diff = weights(r, hp, b, e)
                mix = (gd[b] * jnp.exp(jnp.minimum(diff, 0.0))).astype(BF16)
                ya += dot(mix, one_head(xp, e))
                mixt = (gdt[b] * jnp.exp(jnp.minimum(-diff, 0.0))).astype(BF16)
                da += dot(mixt, one_head(dyp, e))
            yacc[rs, cols] = ya
            dxacc[rs, cols] = da

    def across(c):
        cols = pl.ds(pl.multiple_of(256 * c, 256), 256)
        m = dot(mid2[...], spread(4 * c, 64, 2))
        yacc[256:512, cols] += m[256:512] * dot(g10[...], xe[:, cols])
        dxacc[0:256, cols] += m[0:256] * dot(g10t[...], de[:, cols])

    for c in loads[0:4]:
        c.wait()
    step0(0)
    acc[...] = jnp.zeros_like(acc)
    dg10[...] = jnp.zeros_like(dg10)
    dgd[...] = jnp.zeros_like(dgd)
    dtile[...] = jnp.zeros_like(dtile)
    loads[4].wait()
    whole = tables()
    loads[5].wait()
    loads[6].wait()
    step1(0)
    step0(1)
    loads[7].wait()
    mul(0, [(0, 0), (-1, 0), (1, 0)])
    fwd_b(0, (0,))
    loop(0, 4, dgram_pair)
    step3(0)
    step1(1)
    mul(0, [(0, -1), (0, 1), (2, 0)])
    mul(1, [(0, 0), (-1, 0), (1, 0)])
    fwd_b(0, (-1, 1))
    fwd_b(1, (0,))
    loop(4, 10, dgram_pair)
    fwd_b(0, (2,))
    step3(1)
    loop(0, 4, scaled)
    mul(0, [(-1, -1), (-1, 1), (1, -1), (1, 1)])
    fwd_b(1, (-1, 1))
    mul(1, [(0, -1), (0, 1), (2, 0)])
    loop(4, 8, scaled)
    last(0, (0, -1, 1))
    mul(0, [(2, -1), (2, 1), (0, 2), (-1, 2), (1, 2)])
    fwd_b(1, (2,))
    last(0, (2,))
    mul(0, [(2, 2)])
    bc[:, 0:256] = acc[:, 0:256].astype(BF16)
    states(0, xst, slice(0, 256), ssend, frecv, NEAR)
    mul(1, [(-1, -1), (-1, 1), (1, -1), (1, 1), (2, -1), (2, 1)])
    loop(10, 16, dgram_pair)
    send_decays()
    last(1, (0, -1, 1))
    mul(1, [(0, 2), (-1, 2), (1, 2)])
    last(1, (2,))
    mul(1, [(2, 2)])
    bc[:, 256:512] = acc[:, 256:512].astype(BF16)
    states(1, dyst, slice(256, 512), gsend, grecv, NEAR[0:8])
    dgb[0:256, 0:256] = (dgd[0] * msk[0:256, 0:256]).astype(BF16)
    dgb[256:512, 256:512] = (dgd[1] * msk[256:512, 256:512]).astype(BF16)
    dgb[256:512, 0:256] = (dg10[...] * msk[256:512, 0:256]).astype(BF16)
    dgb[0:256, 256:512] = jnp.zeros((256, 256), BF16)
    b_map, c_map = bc[:, 0:256], bc[:, 256:512]
    row = cnt[0:1, :]
    for b in (0, 1):
        rs = slice(256 * b, 256 * b + 256)
        gd[b] = dot(c_map[rs], b_map[rs], 1, 1) * msk[rs, rs]
        gdt[b] = dot(b_map[rs], c_map[rs], 1, 1) * msk[rs, rs].T
    g10[...] = (dot(c_map[256:512], b_map[0:256], 1, 1) * msk[256:512, 0:256]).astype(BF16)
    g10t[...] = (dot(b_map[0:256], c_map[256:512], 1, 1) * msk[256:512, 0:256].T).astype(BF16)
    acc[:, 0:256] = dot(dgb[...], c_map, 0, 0)
    acc[:, 256:512] = dot(dgb[...], b_map)
    wait_in(4, drecv)
    wait_in(0, frecv)
    wait_out(0, ssend)
    scan(2, frecv, ssend, sin, False)
    states(1, dyst, slice(256, 512), gsend, grecv, NEAR[8:15])
    loop(0, 6, intra_pair)
    wait_in(1, grecv)
    wait_out(1, gsend)
    scan(3, grecv, gsend, rsum, True)
    loop(6, 9, intra_pair)
    def part_of(n):
        g = n // 4
        return 1 - lax.rem(n // 2, 2), lax.rem(2 + 3 * g + 3 * (g // 2) + 2 * (g // 3), 4), lax.rem(n, 2)

    def at_rows(part, at, size):
        return pl.ds(pl.multiple_of(256 * part + at, 128), size)

    def at_cols(half):
        return pl.ds(pl.multiple_of(256 * half, 256), 256)

    def floored(v):
        return jnp.floor(v.astype(F32) * scale + 0.5)

    def msg(n, t, src, dst, axis, sign, half):
        return remote(src, dst, rsend.at[n, t], rrecv.at[n, t], device(half, axis, sign))

    def stage0(n):
        part, da, half = part_of(n)
        k = owner(half, da, 2)
        for t, sign in ((0, 1), (1, -1)):
            src = wbuf.at[k, part, half, 128 * t : 128 * t + 128, :]
            msg(n, t, src, s1.at[n, t], "b", sign, half).start()

    def block_of(part):
        def block(k):
            p = dot(dgb[256 * part : 256 * part + 256, :], hbuf[:, pl.ds(pl.multiple_of(512 * k, 512), 512)])
            top[...] = jnp.maximum(top[...], jnp.max(jnp.abs(p).reshape(32, 8, 512), axis=0))
            wbuf[k, part, 0] = p[:, 0:256].astype(BF16)
            wbuf[k, part, 1] = p[:, 256:512].astype(BF16)

        loop(0, 16, block)

    top[...] = jnp.zeros_like(top)
    for c in sent:
        c.wait_send()
    wait_in(2, sin)
    acc[:, 256:512] += dot(dys[...], sin[...])
    dgb[256:512, :] = acc[:, 256:512].T.astype(BF16)
    block_of(1)
    loop(0, 8, lambda m: stage0(4 * (m // 2) + lax.rem(m, 2)))
    wait_in(3, rsum)
    acc[:, 0:256] += dot(xs[...], rsum[...])
    dgb[0:256, :] = acc[:, 0:256].T.astype(BF16)
    block_of(0)
    def finish_y(c):
        cols = pl.ds(pl.multiple_of(256 * c, 256), 256)
        oh = spread(4 * c, 64, 2)
        c_map, b_map = bc[:, 256:512], bc[:, 0:256]
        for t in (0, 1):
            at = pl.ds(pl.multiple_of(256 * c + 128 * t, 128), 128)
            hs = slice(128 * t, 128 * t + 128)
            carry = dot(c_map, sin[at, :], 1, 1) * dot(ent2[...], oh[:, hs])
            hbuf[:, at] = (yacc[:, at] + carry).astype(BF16)
            carry = dot(b_map, rsum[at, :], 1, 1) * dot(end2[...], oh[:, hs])
            hbuf[:, pl.ds(pl.multiple_of(2048 + 256 * c + 128 * t, 128), 128)] = (dxacc[:, at] + carry).astype(BF16)

    def ship_max(kind, peers):
        for n, dev in enumerate(peers):
            remote(box.at[17 * kind], box.at[17 * kind + 1 + n], msend.at[kind], mrecv.at[kind], dev).start()

    def best_of(kind, peers):
        every = box.at[pl.ds(17 * kind + 1, len(peers))]
        remote(every, every, msend.at[kind], mrecv.at[kind], peers[0]).wait()
        best = box[17 * kind]
        for n in range(len(peers)):
            best = jnp.maximum(best, box[17 * kind + 1 + n])
        return best

    along_seq = [(owner(1, dx, dyy), j) for dx, dyy in NEAR[::-1]]
    along_mp = [(i, lax.rem(j + d, 8)) for d in (4, 3, 5, 2, 6, 1, 7)]
    most = top[:, 0:128]
    for c in range(1, 4):
        most = jnp.maximum(most, top[:, 128 * c : 128 * c + 128])
    box[0] = most
    ship_max(0, along_seq)
    loop(9, 13, intra_pair)
    box[17] = best_of(0, along_seq)
    ship_max(1, along_mp)
    loop(0, 8, lambda m: stage0(4 * (m // 2) + 2 + lax.rem(m, 2)))
    loop(13, 16, intra_pair)
    for kind, src in ((2, ssend), (3, gsend), (4, dtile)):
        wait_out(kind, src)
    best = jnp.full((8, 128), jnp.max(best_of(1, along_mp)), F32)
    guess = jnp.ceil(jnp.log2(best)).astype(jnp.int32)
    guess = jnp.where(power_of_two(guess) < best, guess + 1, guess)
    guess = jnp.where(power_of_two(guess - 1) >= best, guess - 1, guess)
    exp_out[...] = guess.astype(F32)
    scale = jnp.max(power_of_two(20 - guess))

    def stage1(n):
        part, da, half = part_of(n)
        for t, sign in ((0, 1), (1, -1)):
            piece = wbuf.at[owner(half, da, sign), part, half]
            with_sum = slice(128 * t, 128 * t + 128)
            alone = slice(128 - 128 * t, 256 - 128 * t)
            piece[alone, :] = floored(piece[alone, :]).astype(BF16)
            own = floored(piece[with_sum, :])
            msg(n, t, s1.at[n, t], s1.at[n, t], "b", 1, half).wait_recv()
            piece[with_sum, :] = (own + floored(s1[n, t])).astype(BF16)
            msg(n, 2 + t, piece, f1.at[n, t], "b", sign, half).start()

    def total1(n):
        part, da, half = part_of(n)
        k = owner(half, da, 0)
        own = floored(wbuf[k, part, half])
        for t in (0, 1):
            msg(n, 2 + t, f1.at[n, t], f1.at[n, t], "b", 1, half).wait_recv()
        return k, part, half, own + f1[n, 0].astype(F32) + f1[n, 1].astype(F32)

    def stage2(n):
        k, part, half, total = total1(n)
        wbuf[k, part, half] = total.astype(BF16)

    def stage3(s):
        part, half = 1 - s // 2, lax.rem(s, 2)
        k = owner(half, 2, 0)
        for t, sign in ((0, 1), (1, -1)):
            src = wbuf.at[k, part, half, 128 * t : 128 * t + 128, :]
            msg(16 + s, t, src, s2.at[s, t], "a", sign, half).start()

    def stage4(s):
        part, half = 1 - s // 2, lax.rem(s, 2)
        for t, sign in ((0, 1), (1, -1)):
            piece = wbuf.at[owner(half, sign, 0), part, half]
            rs = slice(128 * t, 128 * t + 128)
            msg(16 + s, t, s2.at[s, t], s2.at[s, t], "a", 1, half).wait_recv()
            piece[rs, :] = (piece[rs, :].astype(F32) + s2[s, t].astype(F32)).astype(BF16)
            msg(16 + s, 2 + t, piece, f2.at[s, t], "a", sign, half).start()

    def stage5(n):
        _, part, half, total = total1(n)
        acc[at_rows(part, 0, 256), at_cols(half)] = total

    def stage6(s):
        part, half = 1 - s // 2, lax.rem(s, 2)
        for t in (0, 1):
            msg(16 + s, 2 + t, f2.at[s, t], f2.at[s, t], "a", 1, half).wait_recv()
        rs, cs = at_rows(part, 0, 256), at_cols(half)
        gm_out[rs, cs] = acc[rs, cs] + f2[s, 0].astype(F32) + f2[s, 1].astype(F32)

    loop(0, 8, stage1)
    loop(0, 8, across)
    loop(0, 4, stage2)
    loop(0, 4, stage3)
    loop(8, 12, stage1)
    loop(0, 4, finish_y)
    loop(4, 8, stage2)
    loop(12, 16, stage1)
    loop(4, 8, finish_y)
    ends = [
        pltpu.make_async_copy(hbuf.at[:, 0:2048], y_out, lsem.at[0]),
        pltpu.make_async_copy(hbuf.at[:, 2048:4096], dx_out, lsem.at[1]),
    ]
    for c in ends:
        c.start()
    loop(8, 12, stage2)
    loop(0, 4, stage4)
    loop(12, 16, stage5)
    def left(n):
        for t in (0, 1):
            msg(n, t, s1.at[0, 0], s1.at[0, 0], "b", 1, 0).wait_send()
            msg(n, 2 + t, f1.at[0, 0], f1.at[0, 0], "b", 1, 0).wait_send()

    loop(0, 16, left)
    loop(0, 4, stage6)
    loop(16, 20, left)
    for c in ends:
        c.wait()


def finish(y_in, dx_in, gm_in, exp_in, y_out, dx_out, gm_out, exp_out, buf, gbuf, gout, sem, out_sem):
    pieces, size = 2, 256
    moves = []
    for a, (src, dst) in enumerate(((y_in, y_out), (dx_in, dx_out))):
        for p in range(pieces):
            rows = pl.ds(size * p, size)
            n = a * pieces + p
            moves.append((
                pltpu.make_async_copy(src.at[rows, :], buf.at[a, rows, :], sem.at[n]),
                pltpu.make_async_copy(buf.at[a, rows, :], dst.at[rows, :], out_sem.at[n]),
            ))
    g_in = pltpu.make_async_copy(gm_in, gbuf, sem.at[2 * pieces])
    g_out = pltpu.make_async_copy(gout, gm_out, out_sem.at[2 * pieces])
    g_in.start()
    for load, _ in moves:
        load.start()
    exp_out[...] = exp_in[0:1, 0:1]
    g_in.wait()
    gout[...] = (gbuf[...] * 2.0 ** -20).T
    g_out.start()
    for load, store in moves:
        load.wait()
        store.start()
    for _, store in moves:
        store.wait()
    g_out.wait()


def mixer(lengths, hidden, w, x, log_decay, dy):
    n = len(PLAN)
    vm = pltpu.VMEM
    anyw = pl.BlockSpec(memory_space=pl.ANY)
    vspec = pl.BlockSpec(memory_space=pltpu.VMEM)
    scratch = [
        vm((32, 512), F32), vm((512, 8192), BF16), vm((16, 2, 2, 256, 256), BF16), vm((512, 512), F32), vm((512, 512), BF16),
        vm((512, 2048), BF16), vm((512, 2048), BF16), vm((512, 2048), BF16), vm((512, 2048), BF16),
        vm((2048, 512), BF16), vm((2048, 512), BF16), vm((256, 2048), BF16), vm((256, 2048), BF16),
        vm((512, 2048), F32), vm((512, 2048), F32),
        vm((512, 128), BF16), vm((128, 512), F32), vm((512, 128), BF16), vm((512, 128), BF16), vm((512, 128), BF16),
        vm((8, 512), F32), vm((512, 512), F32), vm((2, 256, 256), F32), vm((256, 256), F32), vm((512, 512), BF16),
        vm((2, 256, 256), F32), vm((2, 256, 256), F32), vm((256, 256), BF16), vm((256, 256), BF16),
        vm((16, 128, 256), BF16), vm((16, 128, 256), BF16), vm((16, 128, 256), BF16), vm((16, 128, 256), BF16),
        vm((2048, 256), BF16), vm((2048, 256), BF16),
        vm((16, 8, 128), F32), vm((16, 8, 128), F32),
        vm((16, 2, 128, 256), BF16), vm((16, 2, 256, 256), BF16), vm((4, 2, 128, 256), BF16), vm((4, 2, 256, 256), BF16),
        vm((8, 512), F32), vm((32, 8, 128), F32),
        pltpu.SemaphoreType.DMA((8,)), pltpu.SemaphoreType.DMA((2, 2, n)), pltpu.SemaphoreType.DMA((2, 2, n)),
        pltpu.SemaphoreType.DMA((5, 16)), pltpu.SemaphoreType.DMA((5, 16)),
        pltpu.SemaphoreType.DMA((20, 4)), pltpu.SemaphoreType.DMA((20, 4)),
        pltpu.SemaphoreType.DMA((2,)), pltpu.SemaphoreType.DMA((2,)),
    ]
    y, dx, gm, ex = pl.pallas_call(
        kernel,
        out_shape=(
            jax.ShapeDtypeStruct((512, 2048), BF16), jax.ShapeDtypeStruct((512, 2048), BF16),
            jax.ShapeDtypeStruct((512, 512), F32), jax.ShapeDtypeStruct((8, 128), F32),
        ),
        in_specs=[pl.BlockSpec(memory_space=pltpu.SMEM), anyw, anyw, anyw, anyw, anyw],
        out_specs=(anyw, anyw, vspec, vspec),
        scratch_shapes=scratch,
        compiler_params=pltpu.CompilerParams(collective_id=0, has_side_effects=True, vmem_limit_bytes=63 * MB),
        name="mixer",
    )(lengths, log_decay.T, hidden, w, x, dy)
    y, dx, gm, ex = pl.pallas_call(
        finish,
        out_shape=(
            jax.ShapeDtypeStruct((512, 2048), BF16), jax.ShapeDtypeStruct((512, 2048), BF16),
            jax.ShapeDtypeStruct((512, 512), F32), jax.ShapeDtypeStruct((1, 1), F32),
        ),
        in_specs=[anyw, anyw, anyw, vspec],
        out_specs=(anyw, anyw, anyw, vspec),
        scratch_shapes=[
            vm((2, 512, 2048), BF16), vm((512, 512), F32), vm((512, 512), F32),
            pltpu.SemaphoreType.DMA((5,)), pltpu.SemaphoreType.DMA((5,)),
        ],
        compiler_params=pltpu.CompilerParams(vmem_limit_bytes=62 * MB),
        name="finish",
    )(y, dx, gm, ex)
    return y, dx, gm, ex.reshape(())


def solution(mesh):
    in_specs = (P(), P("seq", None), P("seq", "mp"), P("seq", "mp"), P("seq", "mp"), P("seq", "mp"))
    out_specs = (P("seq", "mp"), P("seq", "mp"), P("seq", "mp"), P())
    return jax.shard_map(mixer, mesh=mesh, in_specs=in_specs, out_specs=out_specs, check_vma=False)
```
